32 devices in a mesh: seq: 4 (over z), chan: 8 (over y, x, core).
Axes of the slice: x: 2, y: 2, z: 4, core: 2. Of those that a mesh axis runs over, the one named last changes fastest.
Arguments:
- query_proj: bfloat16 [1024, 1024], P('seq', 'chan'), may hold values from -6 to 6
- key_proj: bfloat16 [1024, 1024], P('seq', 'chan'), may hold values from -6 to 6
- value_proj: bfloat16 [1024, 1024], P('seq', 'chan'), may hold values from -6 to 6
- filter_in: float32 [32, 64], replicated, may hold values from -16 to 16
- filter_bias: float32 [64], replicated, may hold values from -3.140625 to 3.140625
- filter_out: float32 [64, 1024], P(None, 'chan'), may hold values from -0.75 to 0.75
- decay_level: float32 [1024], P('chan'), may hold values from 0 to 1
- skip_gain: float32 [1024], P('chan'), may hold values from -4 to 4
- out_weight: bfloat16 [4096, 1024], P(None, 'chan'), may hold values from -0.25 to 0.25
Outputs:
- mixed: bfloat16 [1024, 4096], P('seq', 'chan')
The draws below stay inside these ranges and needn't reach their ends.
All inputs are finite; a program needn't handle non-finite values.
Results may differ from the reference program's by a relative error of at most 0.019.
Values may be sent and summed in bfloat16 or wider, within the bound.
A program may use at most 64 MiB of HBM per device.

```python
import math
import jax
import jax.numpy as jnp
from jax import lax

CH_DEV = 128
CH = 1024
DOUT = 4096
TOK_DEV = 256
TOKENS = 1024
POS = 32
ORDER = 64
N_SEQ = 4
N_CHAN = 8


def with_spikes(array, own_key, source, target, shards_of, factor):
    def block_of(dim):
        return (jnp.arange(array.shape[dim]) // (array.shape[dim] // shards_of)).reshape((-1,) + (1,) * (array.ndim - 1 - dim))

    first = jax.random.permutation(own_key, shards_of)[block_of(target)]
    second = (block_of(target) + shards_of // 2) % shards_of
    return jnp.where((block_of(source) == first) | (block_of(source) == second), factor * array, array)


def block_levels(rng, extent, pieces, smallest, largest):
    loudness, own = 1.0, jax.random.fold_in(rng, 6)
    for axis_at, parts in pieces:
        steps = jnp.exp(jax.random.uniform(jax.random.fold_in(own, axis_at), (parts,), jnp.float32, smallest / len(pieces), largest / len(pieces)))
        loudness = loudness * jnp.repeat(steps, extent[axis_at] // parts).reshape([-1 if axis == axis_at else 1 for axis in range(len(extent))])
    return loudness


def gaussian(stream_key, extent, scale, bound, split=(), kind=jnp.bfloat16):
    array = jax.random.normal(stream_key, extent, jnp.float32) * scale
    if len(split) > 0:
        array = block_levels(stream_key, extent, split, -0.22, 0.18) * array
    return jnp.clip(array, min=-bound, max=bound).astype(kind)


def bell_draw_with(rng, dims, deviation, reach, shards, heavy, held_as=jnp.bfloat16):
    result = deviation * jax.random.normal(rng, dims, jnp.float32)
    if shards:
        result = result * block_levels(rng, dims, shards, -0.22, 0.18)
    return jnp.clip(with_spikes(result, jax.random.fold_in(rng, 3), *heavy), -reach, reach).astype(held_as)


def setup_inputs(seed: int = 0) -> dict:
    seeds = jax.random.split(jax.random.key(seed), 10)
    return {
        "query_proj": gaussian(seeds[0], (TOKENS, CH), 1.0, 6.0, ((0, 4), (1, 8))),
        "key_proj": gaussian(seeds[1], (TOKENS, CH), 1.0, 6.0, ((0, 4), (1, 8))),
        "value_proj": gaussian(seeds[2], (TOKENS, CH), 1.0, 6.0, ((0, 4), (1, 8))),
        "filter_in": jnp.clip(jax.random.uniform(seeds[3], (POS, ORDER), jnp.float32, -16.0, 16.0), -16.0, 16.0),
        "filter_bias": jnp.clip(jax.random.uniform(seeds[4], (ORDER,), jnp.float32, -3.140625, 3.140625), -3.140625, 3.140625),
        "filter_out": gaussian(seeds[5], (ORDER, CH), ORDER ** -0.5, 0.75, ((1, 8),), jnp.float32),
        "decay_level": jnp.clip(1.0 * jax.random.uniform(seeds[6], (CH,), jnp.float32) ** block_levels(seeds[6], (CH,), ((0, 8),), -0.2, 0.2), 0.0, 1.0),
        "skip_gain": gaussian(seeds[7], (CH,), 1.0, 4.0, ((0, 8),), jnp.float32),
        "out_weight": bell_draw_with(seeds[8], (DOUT, CH), CH ** -0.5, 0.25, ((1, 8),), (1, 0, 8, 2.0)),
    }


full_turn = 2.0 * math.pi

def generate(filter_in, filter_bias, filter_out, decay_level, length):
    half_count = POS // 2
    steps_int = jnp.arange(length, dtype=jnp.int32)
    frequency = jnp.arange(1, half_count + 1, dtype=jnp.int32)
    phases = (steps_int[:, None] * frequency[None, :] % length).astype(jnp.float32) * (full_turn / length)
    features = jnp.concatenate([jnp.sin(phases), jnp.cos(phases)], axis=1)
    hidden = jnp.sin(jnp.dot(features, filter_in, precision=lax.Precision.HIGHEST) + filter_bias)
    raw_values = jnp.dot(hidden, filter_out, precision=lax.Precision.HIGHEST)
    levels = jnp.maximum(2.0 * decay_level - 1.0, 0.0)
    decay_rate = 0.5 / length * jnp.exp(levels * math.log(length / 16.0))
    positions = steps_int.astype(jnp.float32)
    return raw_values * jnp.exp(-decay_rate[None, :] * positions[:, None])

def reference(query_proj, key_proj, value_proj, filter_in, filter_bias, filter_out, decay_level, skip_gain, out_weight):
    length = TOK_DEV * N_SEQ
    raw_taps = generate(filter_in, filter_bias, filter_out, decay_level, length)
    filter_taps = raw_taps / jnp.sqrt(lax.optimization_barrier(jnp.sum(raw_taps * raw_taps, axis=0)) + 1e-05)
    mixed_in = key_proj.astype(jnp.float32) * value_proj.astype(jnp.float32)
    spec_in = jnp.fft.rfft(mixed_in, n=2 * length, axis=0)
    spec_taps = jnp.fft.rfft(filter_taps, n=2 * length, axis=0)
    convolved = jnp.fft.irfft(spec_in * spec_taps, n=2 * length, axis=0)[:length]
    gated_rows = (query_proj.astype(jnp.float32) * (convolved + skip_gain[None, :] * mixed_in)).astype(jnp.bfloat16)
    slabs_in = gated_rows.reshape(length, N_CHAN, CH_DEV).transpose(1, 0, 2)
    slabs_weight = out_weight.reshape(DOUT, N_CHAN, CH_DEV).transpose(1, 0, 2)

    def accumulate(running_sum, slab_pair):
        partial_sum = jnp.dot(slab_pair[0], slab_pair[1].T, preferred_element_type=jnp.float32)
        rounded = lax.optimization_barrier(partial_sum.astype(jnp.bfloat16))
        return (running_sum + rounded.astype(jnp.float32), None)
    running_sum, unused = lax.scan(accumulate, jnp.zeros((length, DOUT), jnp.float32), (slabs_in, slabs_weight))
    return running_sum.astype(jnp.bfloat16)
```

```python
import functools
import math

import jax
import jax.numpy as jnp
import numpy as np
from jax import lax
from jax.experimental import pallas as pl
from jax.experimental.pallas import tpu as pltpu
from jax.sharding import PartitionSpec as P

MESH = pl.DeviceIdType.MESH
highest = lax.Precision.HIGHEST


def flipped(index, mask):
    bit, result = 1, index
    while bit <= mask:
        if mask & bit:
            result = result + bit - 2 * bit * ((index // bit) % 2)
        bit *= 2
    return result


def dft_tables(rows):
    freq = np.arange(rows)[:, None]
    size = 2 * rows

    def packed(times):
        angles = (freq * times[None, :] % size) * (2.0 * math.pi / size)
        sines = np.sin(angles)
        sines[0] = 1.0 - 2.0 * (times % 2)
        return np.concatenate([np.cos(angles), sines], axis=0)

    forward = packed(np.arange(rows))
    weight = np.full((2 * rows, 1), 2.0 / size)
    weight[0] = weight[rows] = 1.0 / size
    inverse = (packed(np.arange(rows, size)) * weight * size).T
    return forward, inverse


def feature_table(half_count, seq_count, rows):
    length = seq_count * rows
    freq = np.arange(1, half_count + 1)
    phases = (np.arange(length)[:, None] * freq[None, :] % length) * (2.0 * math.pi / length)
    table = np.concatenate([np.sin(phases), np.cos(phases)], axis=1)
    return table.reshape(seq_count, rows, 2 * half_count)


def sin_turns(turns):
    angle = (turns - jnp.round(turns)) * (2.0 * math.pi)
    square = angle * angle
    total = jnp.full_like(angle, 1.0 / math.factorial(17))
    for order in (15, 13, 11, 9, 7, 5, 3, 1):
        sign = -1.0 if order % 4 == 3 else 1.0
        total = total * square + sign / math.factorial(order)
    return total * angle


def kernel(
    n_seq,
    n_chan,
    q_ref,
    k_ref,
    v_ref,
    fin_ref,
    bias_ref,
    fout_ref,
    level_ref,
    skip_ref,
    feat_ref,
    fwd_ref,
    inv_ref,
    w_ref,
    out_ref,
    x_buf,
    g_buf,
    w_buf,
    spec,
    acc,
    x_send,
    x_recv,
    g_send,
    g_recv,
    w_send,
    w_recv,
    own_sem,
):
    rows, cols = q_ref.shape
    length = rows * n_seq
    width = w_buf.shape[1]
    me_seq = lax.axis_index("seq")
    me_chan = lax.axis_index("chan")

    barrier = pltpu.get_barrier_semaphore()
    for step in range(1, n_seq):
        pl.semaphore_signal(
            barrier, inc=1, device_id={"seq": lax.rem(me_seq + step, n_seq)}, device_id_type=MESH
        )
    for mask in range(1, n_chan):
        pl.semaphore_signal(
            barrier, inc=1, device_id={"chan": flipped(me_chan, mask)}, device_id_type=MESH
        )

    own_weight = pltpu.make_async_copy(
        w_ref.at[pl.ds(pl.multiple_of(me_chan * width, width), width)], w_buf.at[0], own_sem
    )
    own_weight.start()
    mixed_in = k_ref[...].astype(jnp.float32) * v_ref[...].astype(jnp.float32)
    x_buf[0] = mixed_in.astype(jnp.bfloat16)

    def x_copy(step):
        return pltpu.make_async_remote_copy(
            src_ref=x_buf.at[0],
            dst_ref=x_buf.at[step],
            send_sem=x_send.at[step],
            recv_sem=x_recv.at[step],
            device_id={"seq": lax.rem(me_seq + step, n_seq)},
            device_id_type=MESH,
        )

    def w_copy(mask):
        peer = flipped(me_chan, mask)
        return pltpu.make_async_remote_copy(
            src_ref=w_ref.at[pl.ds(pl.multiple_of(peer * width, width), width)],
            dst_ref=w_buf.at[mask],
            send_sem=w_send.at[mask],
            recv_sem=w_recv.at[mask],
            device_id={"chan": peer},
            device_id_type=MESH,
        )

    def g_copy(mask):
        return pltpu.make_async_remote_copy(
            src_ref=g_buf.at[0],
            dst_ref=g_buf.at[mask],
            send_sem=g_send.at[mask],
            recv_sem=g_recv.at[mask],
            device_id={"chan": flipped(me_chan, mask)},
            device_id_type=MESH,
        )

    pl.semaphore_wait(barrier, n_seq + n_chan - 2)
    for step in range(1, n_seq):
        pl.when(me_seq + step < n_seq)(lambda step=step: x_copy(step).start())
    for mask in reversed(range(1, n_chan)):
        w_copy(mask).start()

    levels = jnp.maximum(2.0 * level_ref[...] - 1.0, 0.0)
    rate = 0.5 / length * jnp.exp(levels * math.log(length / 16.0))
    fin = fin_ref[...] * (0.5 / math.pi)
    bias = bias_ref[...] * (0.5 / math.pi)
    fout = fout_ref[...]

    def tap_block(block, squares):
        turns = jnp.dot(
            feat_ref[block], fin, precision=highest, preferred_element_type=jnp.float32
        )
        hidden = sin_turns(turns + bias)
        raw = jnp.dot(hidden, fout, precision=highest, preferred_element_type=jnp.float32)
        place = lax.broadcasted_iota(jnp.int32, (rows, cols), 0) + block * rows
        taps = raw * jnp.exp(-rate * place.astype(jnp.float32))
        spec[block + 1] = jnp.dot(
            fwd_ref[...], taps.astype(jnp.bfloat16), preferred_element_type=jnp.float32
        )
        return squares + jnp.sum(taps * taps, axis=0, keepdims=True)

    spec[0] = jnp.zeros_like(spec[0])
    squares = jnp.zeros((1, cols), jnp.float32)
    if n_seq <= 4:
        for block in range(n_seq):
            squares = tap_block(block, squares)
    else:
        squares = lax.fori_loop(0, n_seq, tap_block, squares)
    scale = lax.rsqrt(squares + 1e-05)

    row_index = lax.broadcasted_iota(jnp.int32, (rows, cols), 0)
    alternate = (1 - 2 * (row_index % 2)).astype(jnp.float32)

    def add_block(step):
        if step > 0:
            x_copy(step).wait_recv()
        field = jnp.dot(fwd_ref[...], x_buf[step], preferred_element_type=jnp.float32)
        x_cos, x_sin = field[:rows], field[rows:]
        h_cos = spec[step, :rows] + alternate * spec[step + 1, :rows]
        h_sin = spec[step, rows:] + alternate * spec[step + 1, rows:]
        terms = (x_cos * h_cos, x_sin * h_sin, x_cos * h_sin + x_sin * h_cos)
        for place, term in enumerate(terms):
            acc[place] = term if step == 0 else acc[place] + term

    for step in range(n_seq):
        if step == 0:
            add_block(step)
        else:
            pl.when(me_seq >= step)(lambda step=step: add_block(step))

    edge = row_index == 0
    y_cos = acc[0] - jnp.where(edge, 0.0, acc[1])
    y_sin = jnp.where(edge, acc[1], acc[2])
    field = jnp.concatenate([y_cos, y_sin], axis=0) * (0.5 / rows)
    convolved = jnp.dot(
        inv_ref[...], field.astype(jnp.bfloat16), preferred_element_type=jnp.float32
    )
    mixed_in = k_ref[...].astype(jnp.float32) * v_ref[...].astype(jnp.float32)
    gated = q_ref[...].astype(jnp.float32) * (convolved * scale + skip_ref[...] * mixed_in)
    g_buf[0] = gated.astype(jnp.bfloat16)
    for mask in reversed(range(1, n_chan)):
        g_copy(mask).start()

    own_weight.wait()
    total = None
    for pair in range(0, n_chan, 2):
        for mask in (pair, pair + 1):
            if mask > 0:
                w_copy(mask).wait_recv()
                g_copy(mask).wait_recv()
        left = jnp.concatenate([g_buf[pair], g_buf[pair + 1]], axis=1)
        right = jnp.concatenate([w_buf[pair], w_buf[pair + 1]], axis=1)
        part = lax.dot_general(
            left, right, (((1,), (1,)), ((), ())), preferred_element_type=jnp.float32
        )
        total = part if total is None else total + part
    out_ref[...] = total.astype(out_ref.dtype)

    for step in range(1, n_seq):
        pl.when(me_seq + step < n_seq)(lambda step=step: x_copy(step).wait_send())
    for mask in range(1, n_chan):
        w_copy(mask).wait_send()
        g_copy(mask).wait_send()


def solution(mesh):
    n_seq, n_chan = mesh.shape["seq"], mesh.shape["chan"]

    def body(query, key, value, fin, bias, fout, level, skip, weight):
        rows, cols = query.shape
        width = weight.shape[0] // n_chan
        forward, inverse = dft_tables(rows)
        features = feature_table(fin.shape[0] // 2, n_seq, rows)
        vmem = pl.BlockSpec(memory_space=pltpu.VMEM)
        return pl.pallas_call(
            functools.partial(kernel, n_seq, n_chan),
            out_shape=jax.ShapeDtypeStruct((rows, width), jnp.bfloat16),
            in_specs=[vmem] * 11 + [pl.BlockSpec(memory_space=pl.ANY)],
            out_specs=vmem,
            scratch_shapes=[
                pltpu.VMEM((n_seq, rows, cols), jnp.bfloat16),
                pltpu.VMEM((n_chan, rows, cols), jnp.bfloat16),
                pltpu.VMEM((n_chan, width, cols), jnp.bfloat16),
                pltpu.VMEM((n_seq + 1, 2 * rows, cols), jnp.float32),
                pltpu.VMEM((3, rows, cols), jnp.float32),
                pltpu.SemaphoreType.DMA((n_seq,)),
                pltpu.SemaphoreType.DMA((n_seq,)),
                pltpu.SemaphoreType.DMA((n_chan,)),
                pltpu.SemaphoreType.DMA((n_chan,)),
                pltpu.SemaphoreType.DMA((n_chan,)),
                pltpu.SemaphoreType.DMA((n_chan,)),
                pltpu.SemaphoreType.DMA,
            ],
            compiler_params=pltpu.CompilerParams(
                collective_id=0, has_side_effects=True, vmem_limit_bytes=40 * 1024 * 1024
            ),
        )(
            query,
            key,
            value,
            fin,
            bias.reshape(1, -1),
            fout,
            level.reshape(1, -1),
            skip.reshape(1, -1),
            jnp.asarray(features, jnp.float32),
            jnp.asarray(forward, jnp.bfloat16),
            jnp.asarray(inverse, jnp.bfloat16),
            weight,
        )

    placed = (
        P("seq", "chan"),
        P("seq", "chan"),
        P("seq", "chan"),
        P(),
        P(),
        P(None, "chan"),
        P("chan"),
        P("chan"),
        P(None, "chan"),
    )
    return jax.shard_map(
        body, mesh=mesh, in_specs=placed, out_specs=P("seq", "chan"), check_vma=False
    )
```

```python
import functools
import math

import jax
import jax.numpy as jnp
import numpy as np
from jax import lax
from jax.experimental import pallas as pl
from jax.experimental.pallas import tpu as pltpu
from jax.sharding import PartitionSpec as P

MESH = pl.DeviceIdType.MESH
highest = lax.Precision.HIGHEST


def flipped(index, mask):
    bit, result = 1, index
    while bit <= mask:
        if mask & bit:
            result = result + bit - 2 * bit * ((index // bit) % 2)
        bit *= 2
    return result


def dft_tables(rows):
    freq = np.arange(rows)[:, None]
    size = 2 * rows

    def packed(times):
        angles = (freq * times[None, :] % size) * (2.0 * math.pi / size)
        sines = np.sin(angles)
        sines[0] = 1.0 - 2.0 * (times % 2)
        return np.concatenate([np.cos(angles), sines], axis=0)

    forward = packed(np.arange(rows))
    weight = np.full((2 * rows, 1), 2.0 / size)
    weight[0] = weight[rows] = 1.0 / size
    inverse = (packed(np.arange(rows, size)) * weight * size).T
    return forward, inverse


def feature_table(half_count, seq_count, rows):
    length = seq_count * rows
    freq = np.arange(1, half_count + 1)
    phases = (np.arange(length)[:, None] * freq[None, :] % length) * (2.0 * math.pi / length)
    table = np.concatenate([np.sin(phases), np.cos(phases)], axis=1)
    return table.reshape(seq_count, rows, 2 * half_count)


def sin_turns(turns):
    angle = (turns - jnp.round(turns)) * (2.0 * math.pi)
    square = angle * angle
    total = jnp.full_like(angle, 1.0 / math.factorial(17))
    for order in (15, 13, 11, 9, 7, 5, 3, 1):
        sign = -1.0 if order % 4 == 3 else 1.0
        total = total * square + sign / math.factorial(order)
    return total * angle


def kernel(
    n_seq,
    n_chan,
    k_hbm,
    v_hbm,
    q_hbm,
    feat_hbm,
    fin_hbm,
    bias_hbm,
    fout_hbm,
    level_hbm,
    fwd_hbm,
    skip_hbm,
    inv_hbm,
    w_ref,
    out_ref,
    k_ref,
    v_ref,
    q_ref,
    feat_ref,
    fin_ref,
    bias_ref,
    fout_ref,
    level_ref,
    fwd_ref,
    skip_ref,
    inv_ref,
    load_sem,
    x_buf,
    g_buf,
    w_buf,
    spec,
    acc,
    x_send,
    x_recv,
    g_send,
    g_recv,
    w_send,
    w_recv,
    z_send,
    z_recv,
    own_sem,
):
    rows, cols = q_ref.shape
    length = rows * n_seq
    width = w_buf.shape[1]
    me_seq = lax.axis_index("seq")
    me_chan = lax.axis_index("chan")
    paired = n_chan == 8
    shared = (6, 7) if paired else ()

    barrier = pltpu.get_barrier_semaphore()
    for step in range(1, n_seq):
        pl.semaphore_signal(
            barrier, inc=1, device_id={"seq": lax.rem(me_seq + step, n_seq)}, device_id_type=MESH
        )
    for mask in range(1, n_chan):
        pl.semaphore_signal(
            barrier, inc=1, device_id={"chan": flipped(me_chan, mask)}, device_id_type=MESH
        )

    sources = (
        k_hbm, v_hbm, fin_hbm, feat_hbm, bias_hbm, fout_hbm, level_hbm, fwd_hbm, q_hbm, skip_hbm, inv_hbm
    )
    targets = (
        k_ref, v_ref, fin_ref, feat_ref, bias_ref, fout_ref, level_ref, fwd_ref, q_ref, skip_ref, inv_ref
    )
    loads = [
        pltpu.make_async_copy(source, target, load_sem.at[place])
        for place, (source, target) in enumerate(zip(sources, targets))
    ]
    for load in loads:
        load.start()
    own_weight = pltpu.make_async_copy(
        w_ref.at[pl.ds(pl.multiple_of(me_chan * width, width), width)], w_buf.at[0], own_sem
    )
    own_weight.start()
    loads[0].wait()
    loads[1].wait()
    mixed_in = k_ref[...].astype(jnp.float32) * v_ref[...].astype(jnp.float32)
    x_buf[0] = mixed_in.astype(jnp.bfloat16)

    def x_copy(step):
        return pltpu.make_async_remote_copy(
            src_ref=x_buf.at[0],
            dst_ref=x_buf.at[step],
            send_sem=x_send.at[step],
            recv_sem=x_recv.at[step],
            device_id={"seq": lax.rem(me_seq + step, n_seq)},
            device_id_type=MESH,
        )

    part = width // n_seq

    def w_copy(mask):
        peer = flipped(me_chan, mask)
        if mask in shared:
            start = peer * width + me_seq * part
            source = w_ref.at[pl.ds(pl.multiple_of(start, part), part)]
            target = w_buf.at[mask, pl.ds(pl.multiple_of(me_seq * part, part), part)]
        else:
            source = w_ref.at[pl.ds(pl.multiple_of(peer * width, width), width)]
            target = w_buf.at[mask]
        return pltpu.make_async_remote_copy(
            src_ref=source,
            dst_ref=target,
            send_sem=w_send.at[mask],
            recv_sem=w_recv.at[mask],
            device_id={"chan": peer},
            device_id_type=MESH,
        )

    def z_copy(place, step, arrives=False):
        owner = lax.rem(me_seq + n_seq - step, n_seq) if arrives else me_seq
        piece = w_buf.at[shared[place], pl.ds(pl.multiple_of(owner * part, part), part)]
        return pltpu.make_async_remote_copy(
            src_ref=piece,
            dst_ref=piece,
            send_sem=z_send.at[place, step],
            recv_sem=z_recv.at[place, step],
            device_id={"seq": lax.rem(me_seq + step, n_seq)},
            device_id_type=MESH,
        )

    def g_copy(mask):
        relayed = paired and mask > 1 and mask % 2 == 1
        return pltpu.make_async_remote_copy(
            src_ref=g_buf.at[mask - 1 if relayed else 0],
            dst_ref=g_buf.at[mask],
            send_sem=g_send.at[mask],
            recv_sem=g_recv.at[mask],
            device_id={"chan": flipped(me_chan, 1 if relayed else mask)},
            device_id_type=MESH,
        )

    pl.semaphore_wait(barrier, n_seq + n_chan - 2)
    for step in range(1, n_seq):
        pl.when(me_seq + step < n_seq)(lambda step=step: x_copy(step).start())
    for mask in reversed(range(1, n_chan)):
        w_copy(mask).start()

    for load in loads[2:8]:
        load.wait()
    levels = jnp.maximum(2.0 * level_ref[...] - 1.0, 0.0)
    rate = 0.5 / length * jnp.exp(levels * math.log(length / 16.0))
    fin = fin_ref[...] * (0.5 / math.pi)
    bias = bias_ref[...] * (0.5 / math.pi)
    fout = fout_ref[...]

    def tap_block(block, squares):
        turns = jnp.dot(
            feat_ref[block], fin, precision=highest, preferred_element_type=jnp.float32
        )
        hidden = sin_turns(turns + bias)
        raw = jnp.dot(hidden, fout, precision=highest, preferred_element_type=jnp.float32)
        place = lax.broadcasted_iota(jnp.int32, (rows, cols), 0) + block * rows
        taps = raw * jnp.exp(-rate * place.astype(jnp.float32))
        spec[block + 1] = jnp.dot(
            fwd_ref[...], taps.astype(jnp.bfloat16), preferred_element_type=jnp.float32
        )
        return squares + jnp.sum(taps * taps, axis=0, keepdims=True)

    spec[0] = jnp.zeros_like(spec[0])
    squares = jnp.zeros((1, cols), jnp.float32)
    if n_seq <= 4:
        for block in range(n_seq):
            squares = tap_block(block, squares)
    else:
        squares = lax.fori_loop(0, n_seq, tap_block, squares)
    scale = lax.rsqrt(squares + 1e-05)

    for place, mask in enumerate(shared):
        w_copy(mask).wait_recv()
        for step in range(1, n_seq):
            z_copy(place, step).start()

    row_index = lax.broadcasted_iota(jnp.int32, (rows, cols), 0)
    alternate = (1 - 2 * (row_index % 2)).astype(jnp.float32)

    def add_block(step):
        if step > 0:
            x_copy(step).wait_recv()
        field = jnp.dot(fwd_ref[...], x_buf[step], preferred_element_type=jnp.float32)
        x_cos, x_sin = field[:rows], field[rows:]
        h_cos = spec[step, :rows] + alternate * spec[step + 1, :rows]
        h_sin = spec[step, rows:] + alternate * spec[step + 1, rows:]
        terms = (x_cos * h_cos, x_sin * h_sin, x_cos * h_sin + x_sin * h_cos)
        for place, term in enumerate(terms):
            acc[place] = term if step == 0 else acc[place] + term

    for step in range(n_seq):
        if step == 0:
            add_block(step)
        else:
            pl.when(me_seq >= step)(lambda step=step: add_block(step))

    for load in loads[8:]:
        load.wait()
    edge = row_index == 0
    y_cos = acc[0] - jnp.where(edge, 0.0, acc[1])
    y_sin = jnp.where(edge, acc[1], acc[2])
    field = jnp.concatenate([y_cos, y_sin], axis=0) * (0.5 / rows)
    convolved = jnp.dot(
        inv_ref[...], field.astype(jnp.bfloat16), preferred_element_type=jnp.float32
    )
    mixed_in = k_ref[...].astype(jnp.float32) * v_ref[...].astype(jnp.float32)
    gated = q_ref[...].astype(jnp.float32) * (convolved * scale + skip_ref[...] * mixed_in)
    g_buf[0] = gated.astype(jnp.bfloat16)
    far = range(2, n_chan, 2 if paired else 1)
    for mask in reversed(far):
        g_copy(mask).start()
    g_copy(1).start()
    own_weight.wait()
    total = None
    for pair in range(0, n_chan, 2):
        for mask in (pair, pair + 1):
            if mask == 0:
                continue
            if mask in shared:
                for step in range(1, n_seq):
                    z_copy(shared.index(mask), step, True).wait_recv()
            else:
                w_copy(mask).wait_recv()
            if not (paired and mask in far):
                g_copy(mask).wait_recv()
        left = jnp.concatenate([g_buf[pair], g_buf[pair + 1]], axis=1)
        right = jnp.concatenate([w_buf[pair], w_buf[pair + 1]], axis=1)
        product = lax.dot_general(
            left, right, (((1,), (1,)), ((), ())), preferred_element_type=jnp.float32
        )
        total = product if total is None else total + product
        if paired and pair == 0:
            for mask in far:
                g_copy(mask).wait_recv()
                g_copy(mask + 1).start()
    out_ref[...] = total.astype(out_ref.dtype)

    for step in range(1, n_seq):
        pl.when(me_seq + step < n_seq)(lambda step=step: x_copy(step).wait_send())
        for place in range(len(shared)):
            z_copy(place, step).wait_send()
    for mask in range(1, n_chan):
        w_copy(mask).wait_send()
        g_copy(mask).wait_send()


def solution(mesh):
    n_seq, n_chan = mesh.shape["seq"], mesh.shape["chan"]

    def body(query, key, value, fin, bias, fout, level, skip, weight):
        rows, cols = query.shape
        width = weight.shape[0] // n_chan
        forward, inverse = dft_tables(rows)
        features = feature_table(fin.shape[0] // 2, n_seq, rows)
        operands = (
            key,
            value,
            query,
            jnp.asarray(features, jnp.float32),
            fin,
            bias.reshape(1, -1),
            fout,
            level.reshape(1, -1),
            jnp.asarray(forward, jnp.bfloat16),
            skip.reshape(1, -1),
            jnp.asarray(inverse, jnp.bfloat16),
        )
        return pl.pallas_call(
            functools.partial(kernel, n_seq, n_chan),
            out_shape=jax.ShapeDtypeStruct((rows, width), jnp.bfloat16),
            in_specs=[pl.BlockSpec(memory_space=pltpu.HBM)] * (len(operands) + 1),
            out_specs=pl.BlockSpec(memory_space=pltpu.VMEM),
            scratch_shapes=[pltpu.VMEM(item.shape, item.dtype) for item in operands]
            + [
                pltpu.SemaphoreType.DMA((len(operands),)),
                pltpu.VMEM((n_seq, rows, cols), jnp.bfloat16),
                pltpu.VMEM((n_chan, rows, cols), jnp.bfloat16),
                pltpu.VMEM((n_chan, width, cols), jnp.bfloat16),
                pltpu.VMEM((n_seq + 1, 2 * rows, cols), jnp.float32),
                pltpu.VMEM((3, rows, cols), jnp.float32),
                pltpu.SemaphoreType.DMA((n_seq,)),
                pltpu.SemaphoreType.DMA((n_seq,)),
                pltpu.SemaphoreType.DMA((n_chan,)),
                pltpu.SemaphoreType.DMA((n_chan,)),
                pltpu.SemaphoreType.DMA((n_chan,)),
                pltpu.SemaphoreType.DMA((n_chan,)),
                pltpu.SemaphoreType.DMA((2, n_seq)),
                pltpu.SemaphoreType.DMA((2, n_seq)),
                pltpu.SemaphoreType.DMA,
            ],
            compiler_params=pltpu.CompilerParams(
                collective_id=0, has_side_effects=True, vmem_limit_bytes=63 * 1024 * 1024
            ),
        )(*operands, weight)

    placed = (
        P("seq", "chan"),
        P("seq", "chan"),
        P("seq", "chan"),
        P(),
        P(),
        P(None, "chan"),
        P("chan"),
        P("chan"),
        P(None, "chan"),
    )
    return jax.shard_map(
        body, mesh=mesh, in_specs=placed, out_specs=P("seq", "chan"), check_vma=False
    )
```

```python
import functools
import math

import jax
import jax.numpy as jnp
import ml_dtypes
import numpy as np
from jax import lax
from jax.experimental import pallas as pl
from jax.experimental.pallas import tpu as pltpu
from jax.sharding import PartitionSpec as P

MESH = pl.DeviceIdType.MESH
products = ((0, 0), (0, 1), (1, 0), (0, 2), (1, 1), (2, 0))


def flipped(index, mask):
    bit, result = 1, index
    while bit <= mask:
        if mask & bit:
            result = result + bit - 2 * bit * ((index // bit) % 2)
        bit *= 2
    return result


def dft_tables(rows):
    freq = np.arange(rows)[:, None]
    size = 2 * rows

    def packed(times):
        angles = (freq * times[None, :] % size) * (2.0 * math.pi / size)
        sines = np.sin(angles)
        sines[0] = 1.0 - 2.0 * (times % 2)
        return np.concatenate([np.cos(angles), sines], axis=0)

    forward = packed(np.arange(rows))
    weight = np.full((2 * rows, 1), 2.0 / size)
    weight[0] = weight[rows] = 1.0 / size
    inverse = (packed(np.arange(rows, size)) * weight * size).T
    return forward, inverse


def feature_table(half_count, seq_count, rows):
    length = seq_count * rows
    freq = np.arange(1, half_count + 1)
    phases = (np.arange(length)[:, None] * freq[None, :] % length) * (2.0 * math.pi / length)
    table = np.concatenate([np.sin(phases), np.cos(phases)], axis=1).astype(np.float32)
    table = table.reshape(seq_count // 2, 2, rows, 2 * half_count)
    table = np.concatenate([table[:, 0], table[:, 1]], axis=2)
    terms = []
    for unused in range(3):
        terms.append(table.astype(ml_dtypes.bfloat16))
        table = table - terms[-1].astype(np.float32)
    return np.concatenate([terms[left] for left, right in products], axis=2)


def split(value, count):
    terms = []
    for place in range(count):
        terms.append(value.astype(jnp.bfloat16))
        if place + 1 < count:
            value = value - terms[-1].astype(jnp.float32)
    return terms


def twice(block):
    empty = jnp.zeros_like(block)
    return jnp.concatenate(
        [jnp.concatenate([block, empty], axis=1), jnp.concatenate([empty, block], axis=1)], axis=0
    )


def sin_turns(turns):
    angle = (turns - jnp.round(turns)) * (2.0 * math.pi)
    square = angle * angle
    total = jnp.full_like(angle, 1.0 / math.factorial(17))
    for order in (15, 13, 11, 9, 7, 5, 3, 1):
        sign = -1.0 if order % 4 == 3 else 1.0
        total = total * square + sign / math.factorial(order)
    return total * angle


def kernel(
    n_seq,
    n_chan,
    k_hbm,
    v_hbm,
    q_hbm,
    feat_hbm,
    fin_hbm,
    bias_hbm,
    fout_hbm,
    level_hbm,
    fwd_hbm,
    skip_hbm,
    inv_hbm,
    w_ref,
    out_ref,
    k_ref,
    v_ref,
    q_ref,
    feat_ref,
    fin_ref,
    bias_ref,
    fout_ref,
    level_ref,
    fwd_ref,
    skip_ref,
    inv_ref,
    load_sem,
    x_buf,
    g_buf,
    w_buf,
    spec,
    acc,
    x_send,
    x_recv,
    g_send,
    g_recv,
    w_send,
    w_recv,
    z_send,
    z_recv,
    own_sem,
):
    rows, cols = q_ref.shape
    length = rows * n_seq
    width = w_buf.shape[1]
    me_seq = lax.axis_index("seq")
    me_chan = lax.axis_index("chan")
    paired = n_chan == 8
    shared = (6, 7) if paired else ()

    barrier = pltpu.get_barrier_semaphore()
    for step in range(1, n_seq):
        pl.semaphore_signal(
            barrier, inc=1, device_id={"seq": lax.rem(me_seq + step, n_seq)}, device_id_type=MESH
        )
    for mask in range(1, n_chan):
        pl.semaphore_signal(
            barrier, inc=1, device_id={"chan": flipped(me_chan, mask)}, device_id_type=MESH
        )

    sources = (
        k_hbm, v_hbm, fin_hbm, feat_hbm, bias_hbm, fout_hbm, level_hbm, fwd_hbm, q_hbm, skip_hbm, inv_hbm
    )
    targets = (
        k_ref, v_ref, fin_ref, feat_ref, bias_ref, fout_ref, level_ref, fwd_ref, q_ref, skip_ref, inv_ref
    )
    loads = [
        pltpu.make_async_copy(source, target, load_sem.at[place])
        for place, (source, target) in enumerate(zip(sources, targets))
    ]
    for load in loads:
        load.start()
    own_weight = pltpu.make_async_copy(
        w_ref.at[pl.ds(pl.multiple_of(me_chan * width, width), width)], w_buf.at[0], own_sem
    )
    own_weight.start()
    loads[0].wait()
    loads[1].wait()
    mixed_in = k_ref[...].astype(jnp.float32) * v_ref[...].astype(jnp.float32)
    x_buf[0] = mixed_in.astype(jnp.bfloat16)

    def x_copy(step):
        return pltpu.make_async_remote_copy(
            src_ref=x_buf.at[0],
            dst_ref=x_buf.at[step],
            send_sem=x_send.at[step],
            recv_sem=x_recv.at[step],
            device_id={"seq": lax.rem(me_seq + step, n_seq)},
            device_id_type=MESH,
        )

    part = width // n_seq

    def w_copy(mask):
        peer = flipped(me_chan, mask)
        if mask in shared:
            start = peer * width + me_seq * part
            source = w_ref.at[pl.ds(pl.multiple_of(start, part), part)]
            target = w_buf.at[mask, pl.ds(pl.multiple_of(me_seq * part, part), part)]
        else:
            source = w_ref.at[pl.ds(pl.multiple_of(peer * width, width), width)]
            target = w_buf.at[mask]
        return pltpu.make_async_remote_copy(
            src_ref=source,
            dst_ref=target,
            send_sem=w_send.at[mask],
            recv_sem=w_recv.at[mask],
            device_id={"chan": peer},
            device_id_type=MESH,
        )

    def z_copy(place, step, arrives=False):
        owner = lax.rem(me_seq + n_seq - step, n_seq) if arrives else me_seq
        piece = w_buf.at[shared[place], pl.ds(pl.multiple_of(owner * part, part), part)]
        return pltpu.make_async_remote_copy(
            src_ref=piece,
            dst_ref=piece,
            send_sem=z_send.at[place, step],
            recv_sem=z_recv.at[place, step],
            device_id={"seq": lax.rem(me_seq + step, n_seq)},
            device_id_type=MESH,
        )

    def g_copy(mask):
        relayed = paired and mask > 1 and mask % 2 == 1
        return pltpu.make_async_remote_copy(
            src_ref=g_buf.at[mask - 1 if relayed else 0],
            dst_ref=g_buf.at[mask],
            send_sem=g_send.at[mask],
            recv_sem=g_recv.at[mask],
            device_id={"chan": flipped(me_chan, 1 if relayed else mask)},
            device_id_type=MESH,
        )

    pl.semaphore_wait(barrier, n_seq + n_chan - 2)
    for step in range(1, n_seq):
        pl.when(me_seq + step < n_seq)(lambda step=step: x_copy(step).start())
    for mask in (6, 7, 4, 2, 5, 3, 1) if paired else reversed(range(1, n_chan)):
        w_copy(mask).start()

    for load in loads[2:8]:
        load.wait()
    levels = jnp.maximum(2.0 * level_ref[...] - 1.0, 0.0)
    rate = 0.5 / length * jnp.exp(levels * math.log(length / 16.0))
    row_index = lax.broadcasted_iota(jnp.int32, (rows, cols), 0)
    alternate = (1 - 2 * (row_index % 2)).astype(jnp.float32)
    alternate = jnp.concatenate([alternate, alternate], axis=0)
    decay = jnp.exp(-rate * row_index.astype(jnp.float32))
    decay = jnp.concatenate([decay, decay], axis=1)
    bias = bias_ref[...] * (0.5 / math.pi)
    bias = jnp.concatenate([bias, bias], axis=1)
    first = [twice(term) for term in split(fin_ref[...] * (0.5 / math.pi), 3)]
    first = jnp.concatenate([first[right] for left, right in products], axis=0)
    second = [twice(term) for term in split(fout_ref[...], 2)]
    second = jnp.concatenate([second[0], second[0], second[1]], axis=0)

    def tap_pair(pair, squares):
        turns = jnp.dot(feat_ref[pair], first, preferred_element_type=jnp.float32)
        high, low = split(sin_turns(turns + bias), 2)
        hidden = jnp.concatenate([high, low, high], axis=1)
        raw = jnp.dot(hidden, second, preferred_element_type=jnp.float32)
        starts = [rate * -(rows * (2 * pair + side)) for side in (0, 1)]
        taps = raw * (decay * jnp.exp(jnp.concatenate(starts, axis=1)))
        both = jnp.dot(
            fwd_ref[...], taps.astype(jnp.bfloat16), preferred_element_type=jnp.float32
        )
        early, late = both[:, :cols], both[:, cols:]
        spec[2 * pair] += alternate * early
        spec[2 * pair + 1] = early + alternate * late
        if n_seq <= 4:
            if 2 * pair + 2 < n_seq:
                spec[2 * pair + 2] = late
        else:
            pl.when(2 * pair + 2 < n_seq)(lambda: spec.__setitem__(2 * pair + 2, late))
        return squares + jnp.sum(taps * taps, axis=0, keepdims=True)

    spec[0] = jnp.zeros_like(spec[0])
    squares = jnp.zeros((1, 2 * cols), jnp.float32)
    if n_seq <= 4:
        for pair in range(n_seq // 2):
            squares = tap_pair(pair, squares)
    else:
        squares = lax.fori_loop(0, n_seq // 2, tap_pair, squares)
    scale = lax.rsqrt(squares[:, :cols] + squares[:, cols:] + 1e-05)

    for place, mask in enumerate(shared):
        w_copy(mask).wait_recv()
        for step in range(1, n_seq):
            z_copy(place, step).start()

    def add_block(step):
        if step > 0:
            x_copy(step).wait_recv()
        field = jnp.dot(fwd_ref[...], x_buf[step], preferred_element_type=jnp.float32)
        x_cos, x_sin = field[:rows], field[rows:]
        h_cos, h_sin = spec[step, :rows], spec[step, rows:]
        terms = (x_cos * h_cos, x_sin * h_sin, x_cos * h_sin + x_sin * h_cos)
        for place, term in enumerate(terms):
            acc[place] = term if step == 0 else acc[place] + term

    for step in range(n_seq):
        if step == 0:
            add_block(step)
        else:
            pl.when(me_seq >= step)(lambda step=step: add_block(step))

    for load in loads[8:]:
        load.wait()
    edge = row_index == 0
    y_cos = acc[0] - jnp.where(edge, 0.0, acc[1])
    y_sin = jnp.where(edge, acc[1], acc[2])
    field = jnp.concatenate([y_cos, y_sin], axis=0) * (0.5 / rows)
    convolved = jnp.dot(
        inv_ref[...], field.astype(jnp.bfloat16), preferred_element_type=jnp.float32
    )
    mixed_in = k_ref[...].astype(jnp.float32) * v_ref[...].astype(jnp.float32)
    gated = q_ref[...].astype(jnp.float32) * (convolved * scale + skip_ref[...] * mixed_in)
    g_buf[0] = gated.astype(jnp.bfloat16)
    far = range(2, n_chan, 2 if paired else 1)
    for mask in reversed(far):
        g_copy(mask).start()
    g_copy(1).start()
    own_weight.wait()
    total = None
    for pair in range(0, n_chan, 2):
        for mask in (pair, pair + 1):
            if mask == 0:
                continue
            if mask in shared:
                for step in range(1, n_seq):
                    z_copy(shared.index(mask), step, True).wait_recv()
            else:
                w_copy(mask).wait_recv()
            if not (paired and mask in far):
                g_copy(mask).wait_recv()
        left = jnp.concatenate([g_buf[pair], g_buf[pair + 1]], axis=1)
        right = jnp.concatenate([w_buf[pair], w_buf[pair + 1]], axis=1)
        product = lax.dot_general(
            left, right, (((1,), (1,)), ((), ())), preferred_element_type=jnp.float32
        )
        total = product if total is None else total + product
        if paired and pair == 0:
            for mask in far:
                g_copy(mask).wait_recv()
                g_copy(mask + 1).start()
    out_ref[...] = total.astype(out_ref.dtype)

    for step in range(1, n_seq):
        pl.when(me_seq + step < n_seq)(lambda step=step: x_copy(step).wait_send())
        for place in range(len(shared)):
            z_copy(place, step).wait_send()
    for mask in range(1, n_chan):
        w_copy(mask).wait_send()
        g_copy(mask).wait_send()


def solution(mesh):
    n_seq, n_chan = mesh.shape["seq"], mesh.shape["chan"]

    def body(query, key, value, fin, bias, fout, level, skip, weight):
        rows, cols = query.shape
        width = weight.shape[0] // n_chan
        forward, inverse = dft_tables(rows)
        features = feature_table(fin.shape[0] // 2, n_seq, rows)
        operands = (
            key,
            value,
            query,
            jnp.asarray(features),
            fin,
            bias.reshape(1, -1),
            fout,
            level.reshape(1, -1),
            jnp.asarray(forward, jnp.bfloat16),
            skip.reshape(1, -1),
            jnp.asarray(inverse, jnp.bfloat16),
        )
        return pl.pallas_call(
            functools.partial(kernel, n_seq, n_chan),
            out_shape=pltpu.VMEM((rows, width), jnp.bfloat16),
            in_specs=[pl.BlockSpec(memory_space=pltpu.HBM)] * (len(operands) + 1),
            out_specs=pl.BlockSpec(memory_space=pltpu.VMEM),
            scratch_shapes=[pltpu.VMEM(item.shape, item.dtype) for item in operands]
            + [
                pltpu.SemaphoreType.DMA((len(operands),)),
                pltpu.VMEM((n_seq, rows, cols), jnp.bfloat16),
                pltpu.VMEM((n_chan, rows, cols), jnp.bfloat16),
                pltpu.VMEM((n_chan, width, cols), jnp.bfloat16),
                pltpu.VMEM((n_seq, 2 * rows, cols), jnp.float32),
                pltpu.VMEM((3, rows, cols), jnp.float32),
                pltpu.SemaphoreType.DMA((n_seq,)),
                pltpu.SemaphoreType.DMA((n_seq,)),
                pltpu.SemaphoreType.DMA((n_chan,)),
                pltpu.SemaphoreType.DMA((n_chan,)),
                pltpu.SemaphoreType.DMA((n_chan,)),
                pltpu.SemaphoreType.DMA((n_chan,)),
                pltpu.SemaphoreType.DMA((2, n_seq)),
                pltpu.SemaphoreType.DMA((2, n_seq)),
                pltpu.SemaphoreType.DMA,
            ],
            compiler_params=pltpu.CompilerParams(
                collective_id=0, has_side_effects=True, vmem_limit_bytes=63 * 1024 * 1024
            ),
        )(*operands, weight)

    placed = (
        P("seq", "chan"),
        P("seq", "chan"),
        P("seq", "chan"),
        P(),
        P(),
        P(None, "chan"),
        P("chan"),
        P("chan"),
        P(None, "chan"),
    )
    return jax.shard_map(
        body, mesh=mesh, in_specs=placed, out_specs=P("seq", "chan"), check_vma=False
    )
```

```python
import functools
import math

import jax
import jax.numpy as jnp
import ml_dtypes
import numpy as np
from jax import lax
from jax.experimental import pallas as pl
from jax.experimental.pallas import tpu as pltpu
from jax.sharding import PartitionSpec as P

MESH = pl.DeviceIdType.MESH
products = ((0, 0), (0, 1), (1, 0), (0, 2), (1, 1), (2, 0))


def flipped(index, mask):
    bit, result = 1, index
    while bit <= mask:
        if mask & bit:
            result = result + bit - 2 * bit * ((index // bit) % 2)
        bit *= 2
    return result


def dft_tables(rows):
    freq = np.arange(rows)[:, None]
    size = 2 * rows

    def packed(times):
        angles = (freq * times[None, :] % size) * (2.0 * math.pi / size)
        sines = np.sin(angles)
        sines[0] = 1.0 - 2.0 * (times % 2)
        return np.concatenate([np.cos(angles), sines], axis=0)

    forward = packed(np.arange(rows))
    weight = np.full((2 * rows, 1), 2.0 / size)
    weight[0] = weight[rows] = 1.0 / size
    inverse = (packed(np.arange(rows, size)) * weight * size).T
    return forward, inverse


def feature_table(half_count, seq_count, rows):
    length = seq_count * rows
    freq = np.arange(1, half_count + 1)
    phases = (np.arange(length)[:, None] * freq[None, :] % length) * (2.0 * math.pi / length)
    table = np.concatenate([np.sin(phases), np.cos(phases)], axis=1).astype(np.float32)
    table = table.reshape(seq_count // 2, 2, rows, 2 * half_count)
    table = np.concatenate([table[:, 0], table[:, 1]], axis=2)
    terms = []
    for unused in range(3):
        terms.append(table.astype(ml_dtypes.bfloat16))
        table = table - terms[-1].astype(np.float32)
    return np.concatenate([terms[left] for left, right in products], axis=2)


def split(value, count):
    terms = []
    for place in range(count):
        terms.append(value.astype(jnp.bfloat16))
        if place + 1 < count:
            value = value - terms[-1].astype(jnp.float32)
    return terms


def twice(block):
    empty = jnp.zeros_like(block)
    return jnp.concatenate(
        [jnp.concatenate([block, empty], axis=1), jnp.concatenate([empty, block], axis=1)], axis=0
    )


def sin_turns(turns):
    angle = (turns - jnp.round(turns)) * (2.0 * math.pi)
    square = angle * angle
    total = jnp.full_like(angle, 1.0 / math.factorial(17))
    for order in (15, 13, 11, 9, 7, 5, 3, 1):
        sign = -1.0 if order % 4 == 3 else 1.0
        total = total * square + sign / math.factorial(order)
    return total * angle


def kernel(
    n_seq,
    n_chan,
    k_hbm,
    v_hbm,
    q_hbm,
    feat_hbm,
    fin_hbm,
    bias_hbm,
    fout_hbm,
    level_hbm,
    fwd_hbm,
    skip_hbm,
    inv_hbm,
    w_ref,
    out_ref,
    k_ref,
    v_ref,
    q_ref,
    feat_ref,
    fin_ref,
    bias_ref,
    fout_ref,
    level_ref,
    fwd_ref,
    skip_ref,
    inv_ref,
    load_sem,
    x_buf,
    g_buf,
    w_buf,
    spec,
    acc,
    x_send,
    x_recv,
    g_send,
    g_recv,
    w_send,
    w_recv,
    z_send,
    z_recv,
    own_sem,
):
    rows, cols = q_ref.shape
    length = rows * n_seq
    width = w_buf.shape[1]
    me_seq = lax.axis_index("seq")
    me_chan = lax.axis_index("chan")
    paired = n_chan == 8 and n_seq % 2 == 0
    shared = (6, 7) if paired else ()

    barrier = pltpu.get_barrier_semaphore()
    for step in range(1, n_seq):
        pl.semaphore_signal(
            barrier, inc=1, device_id={"seq": lax.rem(me_seq + step, n_seq)}, device_id_type=MESH
        )
    for mask in range(1, n_chan):
        pl.semaphore_signal(
            barrier, inc=1, device_id={"chan": flipped(me_chan, mask)}, device_id_type=MESH
        )

    sources = (
        k_hbm, v_hbm, fin_hbm, feat_hbm, bias_hbm, fout_hbm, level_hbm, fwd_hbm, q_hbm, skip_hbm, inv_hbm
    )
    targets = (
        k_ref, v_ref, fin_ref, feat_ref, bias_ref, fout_ref, level_ref, fwd_ref, q_ref, skip_ref, inv_ref
    )
    loads = [
        pltpu.make_async_copy(source, target, load_sem.at[place])
        for place, (source, target) in enumerate(zip(sources, targets))
    ]
    for load in loads:
        load.start()
    own_weight = pltpu.make_async_copy(
        w_ref.at[pl.ds(pl.multiple_of(me_chan * width, width), width)], w_buf.at[0], own_sem
    )
    own_weight.start()
    loads[0].wait()
    loads[1].wait()
    mixed_in = k_ref[...].astype(jnp.float32) * v_ref[...].astype(jnp.float32)
    x_buf[0] = mixed_in.astype(jnp.bfloat16)

    def x_copy(step):
        return pltpu.make_async_remote_copy(
            src_ref=x_buf.at[0],
            dst_ref=x_buf.at[step],
            send_sem=x_send.at[step],
            recv_sem=x_recv.at[step],
            device_id={"seq": lax.rem(me_seq + step, n_seq)},
            device_id_type=MESH,
        )

    part = width // 2

    def w_copy(mask):
        peer = flipped(me_chan, mask)
        if mask in shared:
            start = peer * width + lax.rem(me_seq, 2) * part
            source = w_ref.at[pl.ds(pl.multiple_of(start, part), part)]
            target = w_buf.at[mask, pl.ds(pl.multiple_of(lax.rem(me_seq, 2) * part, part), part)]
        else:
            source = w_ref.at[pl.ds(pl.multiple_of(peer * width, width), width)]
            target = w_buf.at[mask]
        return pltpu.make_async_remote_copy(
            src_ref=source,
            dst_ref=target,
            send_sem=w_send.at[mask],
            recv_sem=w_recv.at[mask],
            device_id={"chan": peer},
            device_id_type=MESH,
        )

    def z_copy(place, arrives=False):
        half = lax.rem(me_seq + 1, 2) if arrives else lax.rem(me_seq, 2)
        piece = w_buf.at[shared[place], pl.ds(pl.multiple_of(half * part, part), part)]
        return pltpu.make_async_remote_copy(
            src_ref=piece,
            dst_ref=piece,
            send_sem=z_send.at[place],
            recv_sem=z_recv.at[place],
            device_id={"seq": flipped(me_seq, 1)},
            device_id_type=MESH,
        )

    def g_copy(mask):
        relayed = paired and mask > 1 and mask % 2 == 1
        return pltpu.make_async_remote_copy(
            src_ref=g_buf.at[mask - 1 if relayed else 0],
            dst_ref=g_buf.at[mask],
            send_sem=g_send.at[mask],
            recv_sem=g_recv.at[mask],
            device_id={"chan": flipped(me_chan, 1 if relayed else mask)},
            device_id_type=MESH,
        )

    pl.semaphore_wait(barrier, n_seq + n_chan - 2)
    for step in reversed(range(1, n_seq)):
        pl.when(me_seq + step < n_seq)(lambda step=step: x_copy(step).start())
    for mask in (6, 7, 4, 2, 5, 3, 1) if paired else reversed(range(1, n_chan)):
        w_copy(mask).start()

    for load in loads[2:8]:
        load.wait()
    levels = jnp.maximum(2.0 * level_ref[...] - 1.0, 0.0)
    rate = 0.5 / length * jnp.exp(levels * math.log(length / 16.0))
    row_index = lax.broadcasted_iota(jnp.int32, (rows, cols), 0)
    alternate = (1 - 2 * (row_index % 2)).astype(jnp.float32)
    alternate = jnp.concatenate([alternate, alternate], axis=0)
    decay = jnp.exp(-rate * row_index.astype(jnp.float32))
    decay = jnp.concatenate([decay, decay], axis=1)
    bias = bias_ref[...] * (0.5 / math.pi)
    bias = jnp.concatenate([bias, bias], axis=1)
    first = [twice(term) for term in split(fin_ref[...] * (0.5 / math.pi), 3)]
    first = jnp.concatenate([first[right] for left, right in products], axis=0)
    second = [twice(term) for term in split(fout_ref[...], 2)]
    second = jnp.concatenate([second[0], second[0], second[1]], axis=0)

    def tap_pair(pair, squares):
        turns = jnp.dot(feat_ref[pair], first, preferred_element_type=jnp.float32)
        high, low = split(sin_turns(turns + bias), 2)
        hidden = jnp.concatenate([high, low, high], axis=1)
        raw = jnp.dot(hidden, second, preferred_element_type=jnp.float32)
        starts = [rate * -(rows * (2 * pair + side)) for side in (0, 1)]
        taps = raw * (decay * jnp.exp(jnp.concatenate(starts, axis=1)))
        both = jnp.dot(
            fwd_ref[...], taps.astype(jnp.bfloat16), preferred_element_type=jnp.float32
        )
        early, late = both[:, :cols], both[:, cols:]
        spec[2 * pair] += alternate * early
        spec[2 * pair + 1] = early + alternate * late
        if n_seq <= 4:
            if 2 * pair + 2 < n_seq:
                spec[2 * pair + 2] = late
        else:
            pl.when(2 * pair + 2 < n_seq)(lambda: spec.__setitem__(2 * pair + 2, late))
        return squares + jnp.sum(taps * taps, axis=0, keepdims=True)

    spec[0] = jnp.zeros_like(spec[0])
    squares = jnp.zeros((1, 2 * cols), jnp.float32)
    if n_seq <= 4:
        for pair in range(n_seq // 2):
            squares = tap_pair(pair, squares)
    else:
        squares = lax.fori_loop(0, n_seq // 2, tap_pair, squares)
    scale = lax.rsqrt(squares[:, :cols] + squares[:, cols:] + 1e-05)

    def add_block(step):
        if step > 0:
            x_copy(step).wait_recv()
        field = jnp.dot(fwd_ref[...], x_buf[step], preferred_element_type=jnp.float32)
        x_cos, x_sin = field[:rows], field[rows:]
        h_cos, h_sin = spec[step, :rows], spec[step, rows:]
        terms = (x_cos * h_cos, x_sin * h_sin, x_cos * h_sin + x_sin * h_cos)
        for place, term in enumerate(terms):
            acc[place] = term if step == 0 else acc[place] + term

    for step in range(n_seq):
        if step == 0:
            add_block(step)
        else:
            pl.when(me_seq >= step)(lambda step=step: add_block(step))

    for load in loads[8:]:
        load.wait()
    edge = row_index == 0
    y_cos = acc[0] - jnp.where(edge, 0.0, acc[1])
    y_sin = jnp.where(edge, acc[1], acc[2])
    field = jnp.concatenate([y_cos, y_sin], axis=0) * (0.5 / rows)
    convolved = jnp.dot(
        inv_ref[...], field.astype(jnp.bfloat16), preferred_element_type=jnp.float32
    )
    mixed_in = k_ref[...].astype(jnp.float32) * v_ref[...].astype(jnp.float32)
    gated = q_ref[...].astype(jnp.float32) * (convolved * scale + skip_ref[...] * mixed_in)
    g_buf[0] = gated.astype(jnp.bfloat16)
    far = range(2, n_chan, 2 if paired else 1)
    for mask in reversed(far):
        g_copy(mask).start()
    g_copy(1).start()
    for place, mask in enumerate(shared):
        w_copy(mask).wait_recv()
        z_copy(place).start()
    own_weight.wait()
    total = None
    for pair in range(0, n_chan, 2):
        for mask in (pair, pair + 1):
            if mask == 0:
                continue
            if mask in shared:
                z_copy(shared.index(mask), True).wait_recv()
            else:
                w_copy(mask).wait_recv()
            if not (paired and mask in far):
                g_copy(mask).wait_recv()
        left = jnp.concatenate([g_buf[pair], g_buf[pair + 1]], axis=1)
        right = jnp.concatenate([w_buf[pair], w_buf[pair + 1]], axis=1)
        product = lax.dot_general(
            left, right, (((1,), (1,)), ((), ())), preferred_element_type=jnp.float32
        )
        total = product if total is None else total + product
        if paired and pair == 0:
            for mask in far:
                g_copy(mask).wait_recv()
                g_copy(mask + 1).start()
    out_ref[...] = total.astype(out_ref.dtype)

    for step in range(1, n_seq):
        pl.when(me_seq + step < n_seq)(lambda step=step: x_copy(step).wait_send())
    for place in range(len(shared)):
        z_copy(place).wait_send()
    for mask in range(1, n_chan):
        w_copy(mask).wait_send()
        g_copy(mask).wait_send()


def solution(mesh):
    n_seq, n_chan = mesh.shape["seq"], mesh.shape["chan"]

    def body(query, key, value, fin, bias, fout, level, skip, weight):
        rows, cols = query.shape
        width = weight.shape[0] // n_chan
        forward, inverse = dft_tables(rows)
        features = feature_table(fin.shape[0] // 2, n_seq, rows)
        operands = (
            key,
            value,
            query,
            jnp.asarray(features),
            fin,
            bias.reshape(1, -1),
            fout,
            level.reshape(1, -1),
            jnp.asarray(forward, jnp.bfloat16),
            skip.reshape(1, -1),
            jnp.asarray(inverse, jnp.bfloat16),
        )
        return pl.pallas_call(
            functools.partial(kernel, n_seq, n_chan),
            out_shape=pltpu.VMEM((rows, width), jnp.bfloat16),
            in_specs=[pl.BlockSpec(memory_space=pltpu.HBM)] * (len(operands) + 1),
            out_specs=pl.BlockSpec(memory_space=pltpu.VMEM),
            scratch_shapes=[pltpu.VMEM(item.shape, item.dtype) for item in operands]
            + [
                pltpu.SemaphoreType.DMA((len(operands),)),
                pltpu.VMEM((n_seq, rows, cols), jnp.bfloat16),
                pltpu.VMEM((n_chan, rows, cols), jnp.bfloat16),
                pltpu.VMEM((n_chan, width, cols), jnp.bfloat16),
                pltpu.VMEM((n_seq, 2 * rows, cols), jnp.float32),
                pltpu.VMEM((3, rows, cols), jnp.float32),
                pltpu.SemaphoreType.DMA((n_seq,)),
                pltpu.SemaphoreType.DMA((n_seq,)),
                pltpu.SemaphoreType.DMA((n_chan,)),
                pltpu.SemaphoreType.DMA((n_chan,)),
                pltpu.SemaphoreType.DMA((n_chan,)),
                pltpu.SemaphoreType.DMA((n_chan,)),
                pltpu.SemaphoreType.DMA((2,)),
                pltpu.SemaphoreType.DMA((2,)),
                pltpu.SemaphoreType.DMA,
            ],
            compiler_params=pltpu.CompilerParams(
                collective_id=0, has_side_effects=True, vmem_limit_bytes=63 * 1024 * 1024
            ),
        )(*operands, weight)

    placed = (
        P("seq", "chan"),
        P("seq", "chan"),
        P("seq", "chan"),
        P(),
        P(),
        P(None, "chan"),
        P("chan"),
        P("chan"),
        P(None, "chan"),
    )
    return jax.shard_map(
        body, mesh=mesh, in_specs=placed, out_specs=P("seq", "chan"), check_vma=False
    )
```

```python
import functools
import math

import jax
import jax.numpy as jnp
import ml_dtypes
import numpy as np
from jax import lax
from jax.experimental import pallas as pl
from jax.experimental.pallas import tpu as pltpu
from jax.sharding import PartitionSpec as P

MESH = pl.DeviceIdType.MESH
products = ((0, 0), (0, 1), (1, 0), (0, 2), (1, 1), (2, 0))


def flipped(index, mask):
    bit, result = 1, index
    while bit <= mask:
        if mask & bit:
            result = result + bit - 2 * bit * ((index // bit) % 2)
        bit *= 2
    return result


def dft_tables(rows):
    freq = np.arange(rows)[:, None]
    size = 2 * rows

    def packed(times):
        angles = (freq * times[None, :] % size) * (2.0 * math.pi / size)
        sines = np.sin(angles)
        sines[0] = 1.0 - 2.0 * (times % 2)
        return np.concatenate([np.cos(angles), sines], axis=0)

    forward = packed(np.arange(rows))
    weight = np.full((2 * rows, 1), 2.0 / size)
    weight[0] = weight[rows] = 1.0 / size
    inverse = (packed(np.arange(rows, size)) * weight * size).T
    return forward, inverse


def feature_table(half_count, seq_count, rows):
    length = seq_count * rows
    freq = np.arange(1, half_count + 1)
    phases = (np.arange(length)[:, None] * freq[None, :] % length) * (2.0 * math.pi / length)
    table = np.concatenate([np.sin(phases), np.cos(phases)], axis=1).astype(np.float32)
    table = table.reshape(seq_count // 2, 2, rows, 2 * half_count)
    table = np.concatenate([table[:, 0], table[:, 1]], axis=2)
    terms = []
    for unused in range(3):
        terms.append(table.astype(ml_dtypes.bfloat16))
        table = table - terms[-1].astype(np.float32)
    return np.concatenate([terms[left] for left, right in products], axis=2)


def split(value, count):
    terms = []
    for place in range(count):
        terms.append(value.astype(jnp.bfloat16))
        if place + 1 < count:
            value = value - terms[-1].astype(jnp.float32)
    return terms


def twice(block):
    empty = jnp.zeros_like(block)
    return jnp.concatenate(
        [jnp.concatenate([block, empty], axis=1), jnp.concatenate([empty, block], axis=1)], axis=0
    )


def sin_turns(turns):
    angle = (turns - jnp.round(turns)) * (2.0 * math.pi)
    square = angle * angle
    total = jnp.full_like(angle, 1.0 / math.factorial(17))
    for order in (15, 13, 11, 9, 7, 5, 3, 1):
        sign = -1.0 if order % 4 == 3 else 1.0
        total = total * square + sign / math.factorial(order)
    return total * angle


def kernel(
    n_seq,
    n_chan,
    k_hbm,
    v_hbm,
    q_hbm,
    feat_hbm,
    fin_hbm,
    bias_hbm,
    fout_hbm,
    level_hbm,
    fwd_hbm,
    skip_hbm,
    inv_hbm,
    w_ref,
    out_ref,
    k_ref,
    v_ref,
    q_ref,
    feat_ref,
    fin_ref,
    bias_ref,
    fout_ref,
    level_ref,
    fwd_ref,
    skip_ref,
    inv_ref,
    load_sem,
    x_buf,
    g_buf,
    w_buf,
    spec,
    acc,
    x_send,
    x_recv,
    g_send,
    g_recv,
    w_send,
    w_recv,
    z_send,
    z_recv,
    own_sem,
):
    rows, cols = q_ref.shape
    length = rows * n_seq
    width = w_buf.shape[1]
    me_seq = lax.axis_index("seq")
    me_chan = lax.axis_index("chan")
    paired = n_chan == 8 and n_seq % 2 == 0
    fetched = {6: 2, 7: 2, 4: 3, 2: 3, 5: 3, 3: 3} if paired else {}

    barrier = pltpu.get_barrier_semaphore()
    for step in range(1, n_seq):
        pl.semaphore_signal(
            barrier, inc=1, device_id={"seq": lax.rem(me_seq + step, n_seq)}, device_id_type=MESH
        )
    for mask in range(1, n_chan):
        pl.semaphore_signal(
            barrier, inc=1, device_id={"chan": flipped(me_chan, mask)}, device_id_type=MESH
        )

    sources = (
        k_hbm, v_hbm, fin_hbm, feat_hbm, bias_hbm, fout_hbm, level_hbm, fwd_hbm, q_hbm, skip_hbm, inv_hbm
    )
    targets = (
        k_ref, v_ref, fin_ref, feat_ref, bias_ref, fout_ref, level_ref, fwd_ref, q_ref, skip_ref, inv_ref
    )
    loads = [
        pltpu.make_async_copy(source, target, load_sem.at[place])
        for place, (source, target) in enumerate(zip(sources, targets))
    ]
    for load in loads:
        load.start()
    own_weight = pltpu.make_async_copy(
        w_ref.at[pl.ds(pl.multiple_of(me_chan * width, width), width)], w_buf.at[0], own_sem
    )
    own_weight.start()
    loads[0].wait()
    loads[1].wait()
    mixed_in = k_ref[...].astype(jnp.float32) * v_ref[...].astype(jnp.float32)
    x_buf[0] = mixed_in.astype(jnp.bfloat16)

    def x_copy(step):
        return pltpu.make_async_remote_copy(
            src_ref=x_buf.at[0],
            dst_ref=x_buf.at[step],
            send_sem=x_send.at[step],
            recv_sem=x_recv.at[step],
            device_id={"seq": lax.rem(me_seq + step, n_seq)},
            device_id_type=MESH,
        )

    piece = width // 4
    odd = lax.rem(me_seq, 2)

    def block_rows(start, count):
        return pl.ds(pl.multiple_of(start, piece), count)

    def w_copy(mask):
        peer = flipped(me_chan, mask)
        count = fetched.get(mask, 4) * piece
        start = odd * (width - count)
        return pltpu.make_async_remote_copy(
            src_ref=w_ref.at[block_rows(peer * width + start, count)],
            dst_ref=w_buf.at[mask, block_rows(start, count)],
            send_sem=w_send.at[mask],
            recv_sem=w_recv.at[mask],
            device_id={"chan": peer},
            device_id_type=MESH,
        )

    def z_copy(mask, arrives=False):
        count = (4 - fetched[mask]) * piece
        side = 1 - odd if arrives else odd
        part = w_buf.at[mask, block_rows(side * (width - count), count)]
        return pltpu.make_async_remote_copy(
            src_ref=part,
            dst_ref=part,
            send_sem=z_send.at[mask],
            recv_sem=z_recv.at[mask],
            device_id={"seq": flipped(me_seq, 1)},
            device_id_type=MESH,
        )

    def g_copy(mask):
        relayed = paired and mask > 1 and mask % 2 == 1
        return pltpu.make_async_remote_copy(
            src_ref=g_buf.at[mask - 1 if relayed else 0],
            dst_ref=g_buf.at[mask],
            send_sem=g_send.at[mask],
            recv_sem=g_recv.at[mask],
            device_id={"chan": flipped(me_chan, 1 if relayed else mask)},
            device_id_type=MESH,
        )

    pl.semaphore_wait(barrier, n_seq + n_chan - 2)
    for step in reversed(range(1, n_seq)):
        pl.when(me_seq + step < n_seq)(lambda step=step: x_copy(step).start())
    for mask in (6, 7, 4, 2, 5, 3, 1) if paired else reversed(range(1, n_chan)):
        w_copy(mask).start()

    for load in loads[2:8]:
        load.wait()
    levels = jnp.maximum(2.0 * level_ref[...] - 1.0, 0.0)
    rate = 0.5 / length * jnp.exp(levels * math.log(length / 16.0))
    row_index = lax.broadcasted_iota(jnp.int32, (rows, cols), 0)
    alternate = (1 - 2 * (row_index % 2)).astype(jnp.float32)
    alternate = jnp.concatenate([alternate, alternate], axis=0)
    decay = jnp.exp(-rate * row_index.astype(jnp.float32))
    decay = jnp.concatenate([decay, decay], axis=1)
    bias = bias_ref[...] * (0.5 / math.pi)
    bias = jnp.concatenate([bias, bias], axis=1)
    first = [twice(term) for term in split(fin_ref[...] * (0.5 / math.pi), 3)]
    first = jnp.concatenate([first[right] for left, right in products], axis=0)
    second = [twice(term) for term in split(fout_ref[...], 2)]
    second = jnp.concatenate([second[0], second[0], second[1]], axis=0)

    def tap_pair(pair, squares):
        turns = jnp.dot(feat_ref[pair], first, preferred_element_type=jnp.float32)
        high, low = split(sin_turns(turns + bias), 2)
        hidden = jnp.concatenate([high, low, high], axis=1)
        raw = jnp.dot(hidden, second, preferred_element_type=jnp.float32)
        starts = [rate * -(rows * (2 * pair + side)) for side in (0, 1)]
        taps = raw * (decay * jnp.exp(jnp.concatenate(starts, axis=1)))
        both = jnp.dot(
            fwd_ref[...], taps.astype(jnp.bfloat16), preferred_element_type=jnp.float32
        )
        early, late = both[:, :cols], both[:, cols:]
        spec[2 * pair] += alternate * early
        spec[2 * pair + 1] = early + alternate * late
        if n_seq <= 4:
            if 2 * pair + 2 < n_seq:
                spec[2 * pair + 2] = late
        else:
            pl.when(2 * pair + 2 < n_seq)(lambda: spec.__setitem__(2 * pair + 2, late))
        return squares + jnp.sum(taps * taps, axis=0, keepdims=True)

    spec[0] = jnp.zeros_like(spec[0])
    squares = jnp.zeros((1, 2 * cols), jnp.float32)
    if n_seq <= 4:
        for pair in range(n_seq // 2):
            squares = tap_pair(pair, squares)
    else:
        squares = lax.fori_loop(0, n_seq // 2, tap_pair, squares)
    scale = lax.rsqrt(squares[:, :cols] + squares[:, cols:] + 1e-05)

    def add_block(step):
        if step > 0:
            x_copy(step).wait_recv()
        field = jnp.dot(fwd_ref[...], x_buf[step], preferred_element_type=jnp.float32)
        x_cos, x_sin = field[:rows], field[rows:]
        h_cos, h_sin = spec[step, :rows], spec[step, rows:]
        terms = (x_cos * h_cos, x_sin * h_sin, x_cos * h_sin + x_sin * h_cos)
        for place, term in enumerate(terms):
            acc[place] = term if step == 0 else acc[place] + term

    for step in range(n_seq):
        if step == 0:
            add_block(step)
        else:
            pl.when(me_seq >= step)(lambda step=step: add_block(step))

    for load in loads[8:]:
        load.wait()
    edge = row_index == 0
    y_cos = acc[0] - jnp.where(edge, 0.0, acc[1])
    y_sin = jnp.where(edge, acc[1], acc[2])
    field = jnp.concatenate([y_cos, y_sin], axis=0) * (0.5 / rows)
    convolved = jnp.dot(
        inv_ref[...], field.astype(jnp.bfloat16), preferred_element_type=jnp.float32
    )
    mixed_in = k_ref[...].astype(jnp.float32) * v_ref[...].astype(jnp.float32)
    gated = q_ref[...].astype(jnp.float32) * (convolved * scale + skip_ref[...] * mixed_in)
    g_buf[0] = gated.astype(jnp.bfloat16)
    far = range(2, n_chan, 2 if paired else 1)
    for mask in reversed(far):
        g_copy(mask).start()
    g_copy(1).start()
    for step in range(1, n_seq):
        pl.when(me_seq + step < n_seq)(lambda step=step: x_copy(step).wait_send())
    for mask in fetched:
        w_copy(mask).wait_recv()
        z_copy(mask).start()
    own_weight.wait()
    total = None
    for pair in range(0, n_chan, 2):
        for mask in (pair, pair + 1):
            if mask == 0:
                continue
            if mask in fetched:
                z_copy(mask, True).wait_recv()
            else:
                w_copy(mask).wait_recv()
            if not (paired and mask in far):
                g_copy(mask).wait_recv()
        left = jnp.concatenate([g_buf[pair], g_buf[pair + 1]], axis=1)
        right = jnp.concatenate([w_buf[pair], w_buf[pair + 1]], axis=1)
        product = lax.dot_general(
            left, right, (((1,), (1,)), ((), ())), preferred_element_type=jnp.float32
        )
        total = product if total is None else total + product
        if paired and pair == 0:
            for mask in far:
                g_copy(mask).wait_recv()
                g_copy(mask + 1).start()
    out_ref[...] = total.astype(out_ref.dtype)

    for mask in fetched:
        z_copy(mask).wait_send()
    for mask in range(1, n_chan):
        w_copy(mask).wait_send()
        g_copy(mask).wait_send()


def solution(mesh):
    n_seq, n_chan = mesh.shape["seq"], mesh.shape["chan"]

    def body(query, key, value, fin, bias, fout, level, skip, weight):
        rows, cols = query.shape
        width = weight.shape[0] // n_chan
        forward, inverse = dft_tables(rows)
        features = feature_table(fin.shape[0] // 2, n_seq, rows)
        operands = (
            key,
            value,
            query,
            jnp.asarray(features),
            fin,
            bias.reshape(1, -1),
            fout,
            level.reshape(1, -1),
            jnp.asarray(forward, jnp.bfloat16),
            skip.reshape(1, -1),
            jnp.asarray(inverse, jnp.bfloat16),
        )
        return pl.pallas_call(
            functools.partial(kernel, n_seq, n_chan),
            out_shape=pltpu.VMEM((rows, width), jnp.bfloat16),
            in_specs=[pl.BlockSpec(memory_space=pltpu.HBM)] * (len(operands) + 1),
            out_specs=pl.BlockSpec(memory_space=pltpu.VMEM),
            scratch_shapes=[pltpu.VMEM(item.shape, item.dtype) for item in operands]
            + [
                pltpu.SemaphoreType.DMA((len(operands),)),
                pltpu.VMEM((n_seq, rows, cols), jnp.bfloat16),
                pltpu.VMEM((n_chan, rows, cols), jnp.bfloat16),
                pltpu.VMEM((n_chan, width, cols), jnp.bfloat16),
                pltpu.VMEM((n_seq, 2 * rows, cols), jnp.float32),
                pltpu.VMEM((3, rows, cols), jnp.float32),
                pltpu.SemaphoreType.DMA((n_seq,)),
                pltpu.SemaphoreType.DMA((n_seq,)),
                pltpu.SemaphoreType.DMA((n_chan,)),
                pltpu.SemaphoreType.DMA((n_chan,)),
                pltpu.SemaphoreType.DMA((n_chan,)),
                pltpu.SemaphoreType.DMA((n_chan,)),
                pltpu.SemaphoreType.DMA((n_chan,)),
                pltpu.SemaphoreType.DMA((n_chan,)),
                pltpu.SemaphoreType.DMA,
            ],
            compiler_params=pltpu.CompilerParams(
                collective_id=0, has_side_effects=True, vmem_limit_bytes=63 * 1024 * 1024
            ),
        )(*operands, weight)

    placed = (
        P("seq", "chan"),
        P("seq", "chan"),
        P("seq", "chan"),
        P(),
        P(),
        P(None, "chan"),
        P("chan"),
        P("chan"),
        P(None, "chan"),
    )
    return jax.shard_map(
        body, mesh=mesh, in_specs=placed, out_specs=P("seq", "chan"), check_vma=False
    )
```

```python
import functools
import math

import jax
import jax.numpy as jnp
import ml_dtypes
import numpy as np
from jax import lax
from jax.experimental import pallas as pl
from jax.experimental.pallas import tpu as pltpu
from jax.sharding import PartitionSpec as P

MESH = pl.DeviceIdType.MESH
products = ((0, 0), (0, 1), (1, 0), (0, 2), (1, 1), (2, 0))


def flipped(index, mask):
    bit, result = 1, index
    while bit <= mask:
        if mask & bit:
            result = result + bit - 2 * bit * ((index // bit) % 2)
        bit *= 2
    return result


def dft_tables(rows):
    freq = np.arange(rows)[:, None]
    size = 2 * rows

    def packed(times):
        angles = (freq * times[None, :] % size) * (2.0 * math.pi / size)
        sines = np.sin(angles)
        sines[0] = 1.0 - 2.0 * (times % 2)
        return np.concatenate([np.cos(angles), sines], axis=0)

    forward = packed(np.arange(rows))
    weight = np.full((2 * rows, 1), 2.0 / size)
    weight[0] = weight[rows] = 1.0 / size
    inverse = (packed(np.arange(rows, size)) * weight * size).T
    return forward, inverse


def feature_table(half_count, seq_count, rows):
    length = seq_count * rows
    freq = np.arange(1, half_count + 1)
    phases = (np.arange(length)[:, None] * freq[None, :] % length) * (2.0 * math.pi / length)
    table = np.concatenate([np.sin(phases), np.cos(phases)], axis=1).astype(np.float32)
    table = table.reshape(seq_count // 2, 2, rows, 2 * half_count)
    table = np.concatenate([table[:, 0], table[:, 1]], axis=2)
    terms = []
    for unused in range(3):
        terms.append(table.astype(ml_dtypes.bfloat16))
        table = table - terms[-1].astype(np.float32)
    return np.concatenate([terms[left] for left, right in products], axis=2)


def split(value, count):
    terms = []
    for place in range(count):
        terms.append(value.astype(jnp.bfloat16))
        if place + 1 < count:
            value = value - terms[-1].astype(jnp.float32)
    return terms


def twice(block):
    empty = jnp.zeros_like(block)
    return jnp.concatenate(
        [jnp.concatenate([block, empty], axis=1), jnp.concatenate([empty, block], axis=1)], axis=0
    )


def regroup(blocks):
    count, lanes = len(blocks), blocks[0].shape[1]
    width = lanes // count
    group = lax.broadcasted_iota(jnp.int32, blocks[0].shape, 1) // width
    results = []
    for target in range(count):
        result = None
        for place, block in enumerate(blocks):
            shift = (place - target) % count * width
            moved = pltpu.roll(block, shift, 1) if shift else block
            result = moved if result is None else jnp.where(group == place, moved, result)
        results.append(result)
    return results


def spread(value, index, count):
    width = value.shape[1] // count
    group = lax.broadcasted_iota(jnp.int32, value.shape, 1) // width
    chosen = value
    for place in range(1, count):
        chosen = jnp.where(index == place, pltpu.roll(value, (count - place) * width, 1), chosen)
    result = chosen
    for place in range(1, count):
        result = jnp.where(group == place, pltpu.roll(chosen, place * width, 1), result)
    return result


def sin_turns(turns):
    angle = (turns - jnp.round(turns)) * (2.0 * math.pi)
    square = angle * angle
    total = jnp.full_like(angle, 1.0 / math.factorial(17))
    for order in (15, 13, 11, 9, 7, 5, 3, 1):
        sign = -1.0 if order % 4 == 3 else 1.0
        total = total * square + sign / math.factorial(order)
    return total * angle


def kernel(
    n_seq,
    n_chan,
    k_hbm,
    v_hbm,
    q_hbm,
    feat_hbm,
    fin_hbm,
    bias_hbm,
    fout_hbm,
    level_hbm,
    fwd_hbm,
    skip_hbm,
    inv_hbm,
    w_ref,
    out_ref,
    k_ref,
    v_ref,
    q_ref,
    feat_ref,
    fin_ref,
    bias_ref,
    fout_ref,
    level_ref,
    fwd_ref,
    skip_ref,
    inv_ref,
    load_sem,
    x_buf,
    g_buf,
    w_buf,
    spec,
    acc,
    x_send,
    x_recv,
    g_send,
    g_recv,
    w_send,
    w_recv,
    z_send,
    z_recv,
    own_sem,
    e_buf,
    y_send,
    y_recv,
):
    rows, cols = q_ref.shape
    length = rows * n_seq
    width = w_buf.shape[1]
    me_seq = lax.axis_index("seq")
    me_chan = lax.axis_index("chan")
    paired = n_chan == 8 and n_seq % 2 == 0
    fetched = {6: 2, 7: 2, 4: 3, 2: 3, 5: 3, 3: 3} if paired else {}

    barrier = pltpu.get_barrier_semaphore()
    for step in range(1, n_seq):
        pl.semaphore_signal(
            barrier, inc=1, device_id={"seq": lax.rem(me_seq + step, n_seq)}, device_id_type=MESH
        )
    for mask in range(1, n_chan):
        pl.semaphore_signal(
            barrier, inc=1, device_id={"chan": flipped(me_chan, mask)}, device_id_type=MESH
        )

    sources = (
        k_hbm, v_hbm, fin_hbm, feat_hbm, bias_hbm, fout_hbm, level_hbm, fwd_hbm, q_hbm, skip_hbm, inv_hbm
    )
    targets = (
        k_ref, v_ref, fin_ref, feat_ref, bias_ref, fout_ref, level_ref, fwd_ref, q_ref, skip_ref, inv_ref
    )
    loads = [
        pltpu.make_async_copy(source, target, load_sem.at[place])
        for place, (source, target) in enumerate(zip(sources, targets))
    ]
    for load in loads:
        load.start()
    own_weight = pltpu.make_async_copy(
        w_ref.at[pl.ds(pl.multiple_of(me_chan * width, width), width)], w_buf.at[0], own_sem
    )
    own_weight.start()
    loads[0].wait()
    loads[1].wait()
    mixed_in = k_ref[...].astype(jnp.float32) * v_ref[...].astype(jnp.float32)
    swap = n_seq == 4
    slab = rows // n_seq

    def store_pieces(value, place):
        pieces = regroup([value[slab * i : slab * (i + 1)] for i in range(n_seq)])
        for i, piece in enumerate(pieces):
            e_buf[place, i] = piece.astype(jnp.bfloat16)

            @pl.when(me_seq == i)
            def own_piece(i=i):
                e_buf[place + 1, i] = e_buf[place, i]


    def load_pieces(place):
        pieces = regroup([e_buf[place, i].astype(jnp.float32) for i in range(n_seq)])
        return jnp.concatenate(pieces, axis=0)

    def swap_copy(place, step):
        peer = lax.rem(me_seq + step, n_seq)
        return pltpu.make_async_remote_copy(
            src_ref=e_buf.at[place, peer],
            dst_ref=e_buf.at[place + 1, me_seq],
            send_sem=(x_send if place == 0 else y_send).at[step],
            recv_sem=(x_recv if place == 0 else y_recv).at[step],
            device_id={"seq": peer},
            device_id_type=MESH,
        )

    if swap:
        store_pieces(mixed_in, 0)
    else:
        x_buf[0] = mixed_in.astype(jnp.bfloat16)

    def x_copy(step):
        return pltpu.make_async_remote_copy(
            src_ref=x_buf.at[0],
            dst_ref=x_buf.at[step],
            send_sem=x_send.at[step],
            recv_sem=x_recv.at[step],
            device_id={"seq": lax.rem(me_seq + step, n_seq)},
            device_id_type=MESH,
        )

    piece = width // 4
    odd = lax.rem(me_seq, 2)

    def block_rows(start, count):
        return pl.ds(pl.multiple_of(start, piece), count)

    def w_copy(mask):
        peer = flipped(me_chan, mask)
        count = fetched.get(mask, 4) * piece
        start = odd * (width - count)
        return pltpu.make_async_remote_copy(
            src_ref=w_ref.at[block_rows(peer * width + start, count)],
            dst_ref=w_buf.at[mask, block_rows(start, count)],
            send_sem=w_send.at[mask],
            recv_sem=w_recv.at[mask],
            device_id={"chan": peer},
            device_id_type=MESH,
        )

    def z_copy(mask, arrives=False):
        count = (4 - fetched[mask]) * piece
        side = 1 - odd if arrives else odd
        part = w_buf.at[mask, block_rows(side * (width - count), count)]
        return pltpu.make_async_remote_copy(
            src_ref=part,
            dst_ref=part,
            send_sem=z_send.at[mask],
            recv_sem=z_recv.at[mask],
            device_id={"seq": flipped(me_seq, 1)},
            device_id_type=MESH,
        )

    def g_copy(mask):
        relayed = paired and mask > 1 and mask % 2 == 1
        return pltpu.make_async_remote_copy(
            src_ref=g_buf.at[mask - 1 if relayed else 0],
            dst_ref=g_buf.at[mask],
            send_sem=g_send.at[mask],
            recv_sem=g_recv.at[mask],
            device_id={"chan": flipped(me_chan, 1 if relayed else mask)},
            device_id_type=MESH,
        )

    pl.semaphore_wait(barrier, n_seq + n_chan - 2)
    for step in reversed(range(1, n_seq)):
        if swap:
            swap_copy(0, step).start()
            continue
        pl.when(me_seq + step < n_seq)(lambda step=step: x_copy(step).start())
    for mask in (6, 7, 4, 2, 5, 3, 1) if paired else reversed(range(1, n_chan)):
        w_copy(mask).start()

    for load in loads[2:8]:
        load.wait()
    def gathered():
        levels = jnp.maximum(2.0 * level_ref[...] - 1.0, 0.0)
        rate = 0.5 / length * jnp.exp(levels * math.log(length / 16.0))
        row_index = lax.broadcasted_iota(jnp.int32, (rows, cols), 0)
        alternate = (1 - 2 * (row_index % 2)).astype(jnp.float32)
        alternate = jnp.concatenate([alternate, alternate], axis=0)
        decay = jnp.exp(-rate * row_index.astype(jnp.float32))
        decay = jnp.concatenate([decay, decay], axis=1)
        bias = bias_ref[...] * (0.5 / math.pi)
        bias = jnp.concatenate([bias, bias], axis=1)
        first = [twice(term) for term in split(fin_ref[...] * (0.5 / math.pi), 3)]
        first = jnp.concatenate([first[right] for left, right in products], axis=0)
        second = [twice(term) for term in split(fout_ref[...], 2)]
        second = jnp.concatenate([second[0], second[0], second[1]], axis=0)

        def tap_pair(pair, squares):
            turns = jnp.dot(feat_ref[pair], first, preferred_element_type=jnp.float32)
            high, low = split(sin_turns(turns + bias), 2)
            hidden = jnp.concatenate([high, low, high], axis=1)
            raw = jnp.dot(hidden, second, preferred_element_type=jnp.float32)
            starts = [rate * -(rows * (2 * pair + side)) for side in (0, 1)]
            taps = raw * (decay * jnp.exp(jnp.concatenate(starts, axis=1)))
            both = jnp.dot(
                fwd_ref[...], taps.astype(jnp.bfloat16), preferred_element_type=jnp.float32
            )
            early, late = both[:, :cols], both[:, cols:]
            spec[2 * pair] += alternate * early
            spec[2 * pair + 1] = early + alternate * late
            if n_seq <= 4:
                if 2 * pair + 2 < n_seq:
                    spec[2 * pair + 2] = late
            else:
                pl.when(2 * pair + 2 < n_seq)(lambda: spec.__setitem__(2 * pair + 2, late))
            return squares + jnp.sum(taps * taps, axis=0, keepdims=True)

        spec[0] = jnp.zeros_like(spec[0])
        squares = jnp.zeros((1, 2 * cols), jnp.float32)
        if n_seq <= 4:
            for pair in range(n_seq // 2):
                squares = tap_pair(pair, squares)
        else:
            squares = lax.fori_loop(0, n_seq // 2, tap_pair, squares)
        scale = lax.rsqrt(squares[:, :cols] + squares[:, cols:] + 1e-05)

        def add_block(step):
            if step > 0:
                x_copy(step).wait_recv()
            field = jnp.dot(fwd_ref[...], x_buf[step], preferred_element_type=jnp.float32)
            x_cos, x_sin = field[:rows], field[rows:]
            h_cos, h_sin = spec[step, :rows], spec[step, rows:]
            terms = (x_cos * h_cos, x_sin * h_sin, x_cos * h_sin + x_sin * h_cos)
            for place, term in enumerate(terms):
                acc[place] = term if step == 0 else acc[place] + term

        for step in range(n_seq):
            if step == 0:
                add_block(step)
            else:
                pl.when(me_seq >= step)(lambda step=step: add_block(step))

        for load in loads[8:]:
            load.wait()
        edge = row_index == 0
        y_cos = acc[0] - jnp.where(edge, 0.0, acc[1])
        y_sin = jnp.where(edge, acc[1], acc[2])
        field = jnp.concatenate([y_cos, y_sin], axis=0) * (0.5 / rows)
        return scale * jnp.dot(
            inv_ref[...], field.astype(jnp.bfloat16), preferred_element_type=jnp.float32
        )

    def swapped():
        width = cols // n_seq
        lane_group = lax.broadcasted_iota(jnp.int32, (rows, cols), 1) // width
        row_index = lax.broadcasted_iota(jnp.int32, (rows, cols), 0)
        alternate = (1 - 2 * (row_index % 2)).astype(jnp.float32)
        alternate = jnp.concatenate([alternate, alternate], axis=0)
        tall_group = jnp.concatenate([lane_group, lane_group], axis=0)
        level = jnp.broadcast_to(level_ref[...], (8, cols))
        levels = jnp.maximum(2.0 * spread(level, me_seq, n_seq)[:1] - 1.0, 0.0)
        rate = 0.5 / length * jnp.exp(levels * math.log(length / 16.0))
        bias = bias_ref[...] * (0.5 / math.pi)
        bias = jnp.concatenate([bias, bias], axis=1)
        first = [twice(term) for term in split(fin_ref[...] * (0.5 / math.pi), 3)]
        first = jnp.concatenate([first[right] for left, right in products], axis=0)
        fout = spread(fout_ref[...], me_seq, n_seq)
        fout_group = lax.broadcasted_iota(jnp.int32, fout.shape, 1) // width
        fout = jnp.concatenate(
            [jnp.where(fout_group == i, fout, 0.0) for i in range(n_seq)], axis=0
        )
        second = split(fout, 2)
        second = jnp.concatenate([second[0], second[0], second[1]], axis=0)
        highs, lows = [], []
        for pair in range(n_seq // 2):
            turns = jnp.dot(feat_ref[pair], first, preferred_element_type=jnp.float32)
            high, low = split(sin_turns(turns + bias), 2)
            highs.append(high)
            lows.append(low)
        hidden = jnp.concatenate(highs + lows + highs, axis=1)
        raw = jnp.dot(hidden, second, preferred_element_type=jnp.float32)
        taps = raw * jnp.exp(-rate * (row_index + rows * lane_group).astype(jnp.float32))
        squares = jnp.sum(taps * taps, axis=0, keepdims=True)
        squares = jnp.broadcast_to(squares, (8, cols))
        total = squares
        for place in range(1, n_seq):
            total = total + pltpu.roll(squares, place * width, 1)
        scale = lax.rsqrt(total[:1] + 1e-05)
        blocks = jnp.dot(
            fwd_ref[...], taps.astype(jnp.bfloat16), preferred_element_type=jnp.float32
        )
        before = jnp.where(tall_group > 0, pltpu.roll(blocks, width, 1), 0.0)
        window = before + alternate * blocks
        for place in range(n_seq):
            chosen = window
            for target in range(n_seq):
                if target != place:
                    shift = (target - place) % n_seq * width
                    chosen = jnp.where(
                        tall_group == target, pltpu.roll(window, shift, 1), chosen
                    )
            spec[place] = jnp.where(tall_group >= place, chosen, 0.0)
        for step in range(1, n_seq):
            swap_copy(0, step).wait_recv()
        tokens = load_pieces(1).astype(jnp.bfloat16)
        field = jnp.dot(fwd_ref[...], tokens, preferred_element_type=jnp.float32)
        sums = None
        for place in range(n_seq):
            moved = pltpu.roll(field, place * width, 1) if place else field
            x_cos, x_sin = moved[:rows], moved[rows:]
            h_cos, h_sin = spec[place, :rows], spec[place, rows:]
            terms = (x_cos * h_cos, x_sin * h_sin, x_cos * h_sin + x_sin * h_cos)
            sums = terms if sums is None else [a + b for a, b in zip(sums, terms)]
        edge = row_index == 0
        y_cos = sums[0] - jnp.where(edge, 0.0, sums[1])
        y_sin = jnp.where(edge, sums[1], sums[2])
        result = jnp.concatenate([y_cos, y_sin], axis=0) * (0.5 / rows)
        loads[10].wait()
        result = scale * jnp.dot(
            inv_ref[...], result.astype(jnp.bfloat16), preferred_element_type=jnp.float32
        )
        store_pieces(result, 2)
        for step in reversed(range(1, n_seq)):
            swap_copy(2, step).start()
        for load in loads[8:10]:
            load.wait()
        for step in range(1, n_seq):
            swap_copy(2, step).wait_recv()
        return load_pieces(3)

    convolved = swapped() if swap else gathered()
    mixed_in = k_ref[...].astype(jnp.float32) * v_ref[...].astype(jnp.float32)
    gated = q_ref[...].astype(jnp.float32) * (convolved + skip_ref[...] * mixed_in)
    g_buf[0] = gated.astype(jnp.bfloat16)
    far = range(2, n_chan, 2 if paired else 1)
    for mask in reversed(far):
        g_copy(mask).start()
    g_copy(1).start()
    for step in range(1, n_seq):
        if swap:
            swap_copy(0, step).wait_send()
            swap_copy(2, step).wait_send()
            continue
        pl.when(me_seq + step < n_seq)(lambda step=step: x_copy(step).wait_send())
    for mask in fetched:
        w_copy(mask).wait_recv()
        z_copy(mask).start()
    own_weight.wait()
    total = None
    for pair in range(0, n_chan, 2):
        for mask in (pair, pair + 1):
            if mask == 0:
                continue
            if mask in fetched:
                z_copy(mask, True).wait_recv()
            else:
                w_copy(mask).wait_recv()
            if not (paired and mask in far):
                g_copy(mask).wait_recv()
        left = jnp.concatenate([g_buf[pair], g_buf[pair + 1]], axis=1)
        right = jnp.concatenate([w_buf[pair], w_buf[pair + 1]], axis=1)
        product = lax.dot_general(
            left, right, (((1,), (1,)), ((), ())), preferred_element_type=jnp.float32
        )
        total = product if total is None else total + product
        if paired and pair == 0:
            for mask in far:
                g_copy(mask).wait_recv()
                g_copy(mask + 1).start()
    out_ref[...] = total.astype(out_ref.dtype)

    for mask in fetched:
        z_copy(mask).wait_send()
    for mask in range(1, n_chan):
        w_copy(mask).wait_send()
        g_copy(mask).wait_send()


def solution(mesh):
    n_seq, n_chan = mesh.shape["seq"], mesh.shape["chan"]

    def body(query, key, value, fin, bias, fout, level, skip, weight):
        rows, cols = query.shape
        width = weight.shape[0] // n_chan
        forward, inverse = dft_tables(rows)
        features = feature_table(fin.shape[0] // 2, n_seq, rows)
        operands = (
            key,
            value,
            query,
            jnp.asarray(features),
            fin,
            bias.reshape(1, -1),
            fout,
            level.reshape(1, -1),
            jnp.asarray(forward, jnp.bfloat16),
            skip.reshape(1, -1),
            jnp.asarray(inverse, jnp.bfloat16),
        )
        return pl.pallas_call(
            functools.partial(kernel, n_seq, n_chan),
            out_shape=pltpu.VMEM((rows, width), jnp.bfloat16),
            in_specs=[pl.BlockSpec(memory_space=pltpu.HBM)] * (len(operands) + 1),
            out_specs=pl.BlockSpec(memory_space=pltpu.VMEM),
            scratch_shapes=[pltpu.VMEM(item.shape, item.dtype) for item in operands]
            + [
                pltpu.SemaphoreType.DMA((len(operands),)),
                pltpu.VMEM((n_seq, rows, cols), jnp.bfloat16),
                pltpu.VMEM((n_chan, rows, cols), jnp.bfloat16),
                pltpu.VMEM((n_chan, width, cols), jnp.bfloat16),
                pltpu.VMEM((n_seq, 2 * rows, cols), jnp.float32),
                pltpu.VMEM((3, rows, cols), jnp.float32),
                pltpu.SemaphoreType.DMA((n_seq,)),
                pltpu.SemaphoreType.DMA((n_seq,)),
                pltpu.SemaphoreType.DMA((n_chan,)),
                pltpu.SemaphoreType.DMA((n_chan,)),
                pltpu.SemaphoreType.DMA((n_chan,)),
                pltpu.SemaphoreType.DMA((n_chan,)),
                pltpu.SemaphoreType.DMA((n_chan,)),
                pltpu.SemaphoreType.DMA((n_chan,)),
                pltpu.SemaphoreType.DMA,
                pltpu.VMEM((4, n_seq, rows // n_seq, cols), jnp.bfloat16),
                pltpu.SemaphoreType.DMA((n_seq,)),
                pltpu.SemaphoreType.DMA((n_seq,)),
            ],
            compiler_params=pltpu.CompilerParams(
                collective_id=0, has_side_effects=True, vmem_limit_bytes=63 * 1024 * 1024
            ),
        )(*operands, weight)

    placed = (
        P("seq", "chan"),
        P("seq", "chan"),
        P("seq", "chan"),
        P(),
        P(),
        P(None, "chan"),
        P("chan"),
        P("chan"),
        P(None, "chan"),
    )
    return jax.shard_map(
        body, mesh=mesh, in_specs=placed, out_specs=P("seq", "chan"), check_vma=False
    )
```

```python
import functools
import math

import jax
import jax.numpy as jnp
import ml_dtypes
import numpy as np
from jax import lax
from jax.experimental import pallas as pl
from jax.experimental.pallas import tpu as pltpu
from jax.sharding import PartitionSpec as P

MESH = pl.DeviceIdType.MESH
products = ((0, 0), (0, 1), (1, 0), (0, 2), (1, 1), (2, 0))


def flipped(index, mask):
    bit, result = 1, index
    while bit <= mask:
        if mask & bit:
            result = result + bit - 2 * bit * ((index // bit) % 2)
        bit *= 2
    return result


def dft_tables(rows):
    freq = np.arange(rows)[:, None]
    size = 2 * rows

    def packed(times):
        angles = (freq * times[None, :] % size) * (2.0 * math.pi / size)
        sines = np.sin(angles)
        sines[0] = 1.0 - 2.0 * (times % 2)
        return np.concatenate([np.cos(angles), sines], axis=0)

    forward = packed(np.arange(rows))
    weight = np.full((2 * rows, 1), 2.0 / size)
    weight[0] = weight[rows] = 1.0 / size
    inverse = (packed(np.arange(rows, size)) * weight * size).T
    return forward, inverse


def feature_table(half_count, seq_count, rows):
    length = seq_count * rows
    freq = np.arange(1, half_count + 1)
    phases = (np.arange(length)[:, None] * freq[None, :] % length) * (2.0 * math.pi / length)
    table = np.concatenate([np.sin(phases), np.cos(phases)], axis=1).astype(np.float32)
    table = table.reshape(seq_count // 2, 2, rows, 2 * half_count)
    table = np.concatenate([table[:, 0], table[:, 1]], axis=2)
    terms = []
    for unused in range(3):
        terms.append(table.astype(ml_dtypes.bfloat16))
        table = table - terms[-1].astype(np.float32)
    return np.concatenate([terms[left] for left, right in products], axis=2)


def split(value, count):
    terms = []
    for place in range(count):
        terms.append(value.astype(jnp.bfloat16))
        if place + 1 < count:
            value = value - terms[-1].astype(jnp.float32)
    return terms


def twice(block):
    empty = jnp.zeros_like(block)
    return jnp.concatenate(
        [jnp.concatenate([block, empty], axis=1), jnp.concatenate([empty, block], axis=1)], axis=0
    )


def sin_turns(turns):
    angle = (turns - jnp.round(turns)) * (2.0 * math.pi)
    square = angle * angle
    total = jnp.full_like(angle, 1.0 / math.factorial(17))
    for order in (15, 13, 11, 9, 7, 5, 3, 1):
        sign = -1.0 if order % 4 == 3 else 1.0
        total = total * square + sign / math.factorial(order)
    return total * angle


def kernel(
    n_seq,
    n_chan,
    k_hbm,
    v_hbm,
    q_hbm,
    feat_hbm,
    fin_hbm,
    bias_hbm,
    fout_hbm,
    level_hbm,
    fwd_hbm,
    skip_hbm,
    inv_hbm,
    w_ref,
    out_ref,
    k_ref,
    v_ref,
    q_ref,
    feat_ref,
    fin_ref,
    bias_ref,
    fout_ref,
    level_ref,
    fwd_ref,
    skip_ref,
    inv_ref,
    load_sem,
    x_buf,
    g_buf,
    w_buf,
    spec,
    acc,
    x_send,
    x_recv,
    g_send,
    g_recv,
    w_send,
    w_recv,
    z_send,
    z_recv,
    own_sem,
):
    rows, cols = q_ref.shape
    length = rows * n_seq
    width = w_buf.shape[1]
    me_seq = lax.axis_index("seq")
    me_chan = lax.axis_index("chan")
    paired = n_chan == 8 and n_seq % 2 == 0
    fetched = {6: 2, 7: 2, 4: 3, 2: 3, 5: 3, 3: 3} if paired else {}

    barrier = pltpu.get_barrier_semaphore()
    for step in range(1, n_seq):
        pl.semaphore_signal(
            barrier, inc=1, device_id={"seq": lax.rem(me_seq + step, n_seq)}, device_id_type=MESH
        )
    for mask in range(1, n_chan):
        pl.semaphore_signal(
            barrier, inc=1, device_id={"chan": flipped(me_chan, mask)}, device_id_type=MESH
        )

    sources = (
        k_hbm, v_hbm, fin_hbm, feat_hbm, bias_hbm, fout_hbm, level_hbm, fwd_hbm, q_hbm, skip_hbm, inv_hbm
    )
    targets = (
        k_ref, v_ref, fin_ref, feat_ref, bias_ref, fout_ref, level_ref, fwd_ref, q_ref, skip_ref, inv_ref
    )
    loads = [
        pltpu.make_async_copy(source, target, load_sem.at[place])
        for place, (source, target) in enumerate(zip(sources, targets))
    ]
    for load in loads:
        load.start()
    own_weight = pltpu.make_async_copy(
        w_ref.at[pl.ds(pl.multiple_of(me_chan * width, width), width)], w_buf.at[0], own_sem
    )
    own_weight.start()
    loads[0].wait()
    loads[1].wait()
    mixed_in = k_ref[...].astype(jnp.float32) * v_ref[...].astype(jnp.float32)
    x_buf[0] = mixed_in.astype(jnp.bfloat16)

    def x_copy(step):
        return pltpu.make_async_remote_copy(
            src_ref=x_buf.at[0],
            dst_ref=x_buf.at[step],
            send_sem=x_send.at[step],
            recv_sem=x_recv.at[step],
            device_id={"seq": lax.rem(me_seq + step, n_seq)},
            device_id_type=MESH,
        )

    piece = width // 4
    odd = lax.rem(me_seq, 2)

    def block_rows(start, count):
        return pl.ds(pl.multiple_of(start, piece), count)

    def w_copy(mask, first=False):
        peer = flipped(me_chan, mask)
        count = (4 - fetched.get(mask, 4)) * piece
        start = count
        if first:
            start = odd * (width - count)
        else:
            count = width - 2 * count
        place = mask + n_chan if first else mask
        return pltpu.make_async_remote_copy(
            src_ref=w_ref.at[block_rows(peer * width + start, count)],
            dst_ref=w_buf.at[mask, block_rows(start, count)],
            send_sem=w_send.at[place],
            recv_sem=w_recv.at[place],
            device_id={"chan": peer},
            device_id_type=MESH,
        )

    def z_copy(mask, arrives=False):
        count = (4 - fetched[mask]) * piece
        side = 1 - odd if arrives else odd
        part = w_buf.at[mask, block_rows(side * (width - count), count)]
        return pltpu.make_async_remote_copy(
            src_ref=part,
            dst_ref=part,
            send_sem=z_send.at[mask],
            recv_sem=z_recv.at[mask],
            device_id={"seq": flipped(me_seq, 1)},
            device_id_type=MESH,
        )

    def g_copy(mask):
        relayed = paired and mask > 1 and mask % 2 == 1
        return pltpu.make_async_remote_copy(
            src_ref=g_buf.at[mask - 1 if relayed else 0],
            dst_ref=g_buf.at[mask],
            send_sem=g_send.at[mask],
            recv_sem=g_recv.at[mask],
            device_id={"chan": flipped(me_chan, 1 if relayed else mask)},
            device_id_type=MESH,
        )

    pl.semaphore_wait(barrier, n_seq + n_chan - 2)
    for step in reversed(range(1, n_seq)):
        pl.when(me_seq + step < n_seq)(lambda step=step: x_copy(step).start())
    for mask in fetched:
        w_copy(mask, True).start()
    kept = [mask for mask in (4, 2, 5, 3, 1) if paired] or list(reversed(range(1, n_chan)))
    for mask in kept:
        w_copy(mask).start()

    def forward(mask):
        w_copy(mask, True).wait_recv()
        z_copy(mask).start()

    for load in loads[2:8]:
        load.wait()
    levels = jnp.maximum(2.0 * level_ref[...] - 1.0, 0.0)
    rate = 0.5 / length * jnp.exp(levels * math.log(length / 16.0))
    row_index = lax.broadcasted_iota(jnp.int32, (rows, cols), 0)
    alternate = (1 - 2 * (row_index % 2)).astype(jnp.float32)
    alternate = jnp.concatenate([alternate, alternate], axis=0)
    decay = jnp.exp(-rate * row_index.astype(jnp.float32))
    decay = jnp.concatenate([decay, decay], axis=1)
    bias = bias_ref[...] * (0.5 / math.pi)
    bias = jnp.concatenate([bias, bias], axis=1)
    first = [twice(term) for term in split(fin_ref[...] * (0.5 / math.pi), 3)]
    first = jnp.concatenate([first[right] for left, right in products], axis=0)
    second = [twice(term) for term in split(fout_ref[...], 2)]
    second = jnp.concatenate([second[0], second[0], second[1]], axis=0)

    def tap_pair(pair, squares):
        turns = jnp.dot(feat_ref[pair], first, preferred_element_type=jnp.float32)
        high, low = split(sin_turns(turns + bias), 2)
        hidden = jnp.concatenate([high, low, high], axis=1)
        raw = jnp.dot(hidden, second, preferred_element_type=jnp.float32)
        starts = [rate * -(rows * (2 * pair + side)) for side in (0, 1)]
        taps = raw * (decay * jnp.exp(jnp.concatenate(starts, axis=1)))
        both = jnp.dot(
            fwd_ref[...], taps.astype(jnp.bfloat16), preferred_element_type=jnp.float32
        )
        early, late = both[:, :cols], both[:, cols:]
        spec[2 * pair] += alternate * early
        spec[2 * pair + 1] = early + alternate * late
        if n_seq <= 4:
            if 2 * pair + 2 < n_seq:
                spec[2 * pair + 2] = late
        else:
            pl.when(2 * pair + 2 < n_seq)(lambda: spec.__setitem__(2 * pair + 2, late))
        return squares + jnp.sum(taps * taps, axis=0, keepdims=True)

    spec[0] = jnp.zeros_like(spec[0])
    squares = jnp.zeros((1, 2 * cols), jnp.float32)
    if n_seq <= 4:
        for pair in range(n_seq // 2):
            squares = tap_pair(pair, squares)
    else:
        squares = lax.fori_loop(0, n_seq // 2, tap_pair, squares)
    scale = lax.rsqrt(squares[:, :cols] + squares[:, cols:] + 1e-05)

    def add_block(step):
        if step > 0:
            x_copy(step).wait_recv()
        field = jnp.dot(fwd_ref[...], x_buf[step], preferred_element_type=jnp.float32)
        x_cos, x_sin = field[:rows], field[rows:]
        h_cos, h_sin = spec[step, :rows], spec[step, rows:]
        terms = (x_cos * h_cos, x_sin * h_sin, x_cos * h_sin + x_sin * h_cos)
        for place, term in enumerate(terms):
            acc[place] = term if step == 0 else acc[place] + term

    for step in range(n_seq):
        if step == 0:
            add_block(step)
            for mask in fetched:
                if mask not in kept:
                    pl.when(odd == 1)(lambda mask=mask: forward(mask))
        else:
            pl.when(me_seq >= step)(lambda step=step: add_block(step))

    for load in loads[8:]:
        load.wait()
    edge = row_index == 0
    y_cos = acc[0] - jnp.where(edge, 0.0, acc[1])
    y_sin = jnp.where(edge, acc[1], acc[2])
    field = jnp.concatenate([y_cos, y_sin], axis=0) * (0.5 / rows)
    convolved = jnp.dot(
        inv_ref[...], field.astype(jnp.bfloat16), preferred_element_type=jnp.float32
    )
    mixed_in = k_ref[...].astype(jnp.float32) * v_ref[...].astype(jnp.float32)
    gated = q_ref[...].astype(jnp.float32) * (convolved * scale + skip_ref[...] * mixed_in)
    g_buf[0] = gated.astype(jnp.bfloat16)
    far = range(2, n_chan, 2 if paired else 1)
    for mask in reversed(far):
        g_copy(mask).start()
    g_copy(1).start()
    for step in range(1, n_seq):
        pl.when(me_seq + step < n_seq)(lambda step=step: x_copy(step).wait_send())
    for mask in fetched:
        if mask in kept:
            forward(mask)
        else:
            pl.when(odd == 0)(lambda mask=mask: forward(mask))
    own_weight.wait()
    total = None
    for pair in range(0, n_chan, 2):
        for mask in (pair, pair + 1):
            if mask == 0:
                continue
            if mask in fetched:
                z_copy(mask, True).wait_recv()
            if mask in kept:
                w_copy(mask).wait_recv()
            if not (paired and mask in far):
                g_copy(mask).wait_recv()
        left = jnp.concatenate([g_buf[pair], g_buf[pair + 1]], axis=1)
        right = jnp.concatenate([w_buf[pair], w_buf[pair + 1]], axis=1)
        product = lax.dot_general(
            left, right, (((1,), (1,)), ((), ())), preferred_element_type=jnp.float32
        )
        total = product if total is None else total + product
        if paired and pair == 0:
            for mask in far:
                g_copy(mask).wait_recv()
                g_copy(mask + 1).start()
    out_ref[...] = total.astype(out_ref.dtype)

    for mask in fetched:
        z_copy(mask).wait_send()
        w_copy(mask, True).wait_send()
    for mask in range(1, n_chan):
        if mask in kept:
            w_copy(mask).wait_send()
        g_copy(mask).wait_send()


def solution(mesh):
    n_seq, n_chan = mesh.shape["seq"], mesh.shape["chan"]

    def body(query, key, value, fin, bias, fout, level, skip, weight):
        rows, cols = query.shape
        width = weight.shape[0] // n_chan
        forward, inverse = dft_tables(rows)
        features = feature_table(fin.shape[0] // 2, n_seq, rows)
        operands = (
            key,
            value,
            query,
            jnp.asarray(features),
            fin,
            bias.reshape(1, -1),
            fout,
            level.reshape(1, -1),
            jnp.asarray(forward, jnp.bfloat16),
            skip.reshape(1, -1),
            jnp.asarray(inverse, jnp.bfloat16),
        )
        return pl.pallas_call(
            functools.partial(kernel, n_seq, n_chan),
            out_shape=pltpu.VMEM((rows, width), jnp.bfloat16),
            in_specs=[pl.BlockSpec(memory_space=pltpu.HBM)] * (len(operands) + 1),
            out_specs=pl.BlockSpec(memory_space=pltpu.VMEM),
            scratch_shapes=[pltpu.VMEM(item.shape, item.dtype) for item in operands]
            + [
                pltpu.SemaphoreType.DMA((len(operands),)),
                pltpu.VMEM((n_seq, rows, cols), jnp.bfloat16),
                pltpu.VMEM((n_chan, rows, cols), jnp.bfloat16),
                pltpu.VMEM((n_chan, width, cols), jnp.bfloat16),
                pltpu.VMEM((n_seq, 2 * rows, cols), jnp.float32),
                pltpu.VMEM((3, rows, cols), jnp.float32),
                pltpu.SemaphoreType.DMA((n_seq,)),
                pltpu.SemaphoreType.DMA((n_seq,)),
                pltpu.SemaphoreType.DMA((n_chan,)),
                pltpu.SemaphoreType.DMA((n_chan,)),
                pltpu.SemaphoreType.DMA((2 * n_chan,)),
                pltpu.SemaphoreType.DMA((2 * n_chan,)),
                pltpu.SemaphoreType.DMA((n_chan,)),
                pltpu.SemaphoreType.DMA((n_chan,)),
                pltpu.SemaphoreType.DMA,
            ],
            compiler_params=pltpu.CompilerParams(
                collective_id=0, has_side_effects=True, vmem_limit_bytes=63 * 1024 * 1024
            ),
        )(*operands, weight)

    placed = (
        P("seq", "chan"),
        P("seq", "chan"),
        P("seq", "chan"),
        P(),
        P(),
        P(None, "chan"),
        P("chan"),
        P("chan"),
        P(None, "chan"),
    )
    return jax.shard_map(
        body, mesh=mesh, in_specs=placed, out_specs=P("seq", "chan"), check_vma=False
    )
```

```python
import functools
import math

import jax
import jax.numpy as jnp
import ml_dtypes
import numpy as np
from jax import lax
from jax.experimental import pallas as pl
from jax.experimental.pallas import tpu as pltpu
from jax.sharding import PartitionSpec as P

MESH = pl.DeviceIdType.MESH
products = ((0, 0), (0, 1), (1, 0), (0, 2), (1, 1), (2, 0))


def flipped(index, mask):
    bit, result = 1, index
    while bit <= mask:
        if mask & bit:
            result = result + bit - 2 * bit * ((index // bit) % 2)
        bit *= 2
    return result


def dft_tables(rows):
    freq = np.arange(rows)[:, None]
    size = 2 * rows

    def packed(times):
        angles = (freq * times[None, :] % size) * (2.0 * math.pi / size)
        sines = np.sin(angles)
        sines[0] = 1.0 - 2.0 * (times % 2)
        return np.concatenate([np.cos(angles), sines], axis=0)

    forward = packed(np.arange(rows))
    weight = np.full((2 * rows, 1), 2.0 / size)
    weight[0] = weight[rows] = 1.0 / size
    inverse = (packed(np.arange(rows, size)) * weight * size).T
    return forward, inverse


def feature_table(half_count, seq_count, rows):
    length = seq_count * rows
    freq = np.arange(1, half_count + 1)
    phases = (np.arange(length)[:, None] * freq[None, :] % length) * (2.0 * math.pi / length)
    table = np.concatenate([np.sin(phases), np.cos(phases)], axis=1).astype(np.float32)
    table = table.reshape(seq_count // 2, 2, rows, 2 * half_count)
    table = np.concatenate([table[:, 0], table[:, 1]], axis=2)
    terms = []
    for unused in range(3):
        terms.append(table.astype(ml_dtypes.bfloat16))
        table = table - terms[-1].astype(np.float32)
    return np.concatenate([terms[left] for left, right in products], axis=2)


def split(value, count):
    terms = []
    for place in range(count):
        terms.append(value.astype(jnp.bfloat16))
        if place + 1 < count:
            value = value - terms[-1].astype(jnp.float32)
    return terms


def twice(block):
    empty = jnp.zeros_like(block)
    return jnp.concatenate(
        [jnp.concatenate([block, empty], axis=1), jnp.concatenate([empty, block], axis=1)], axis=0
    )


def sin_turns(turns):
    angle = (turns - jnp.round(turns)) * (2.0 * math.pi)
    square = angle * angle
    total = jnp.full_like(angle, 1.0 / math.factorial(17))
    for order in (15, 13, 11, 9, 7, 5, 3, 1):
        sign = -1.0 if order % 4 == 3 else 1.0
        total = total * square + sign / math.factorial(order)
    return total * angle


def kernel(
    n_seq,
    n_chan,
    k_hbm,
    v_hbm,
    q_hbm,
    feat_hbm,
    fin_hbm,
    bias_hbm,
    fout_hbm,
    level_hbm,
    fwd_hbm,
    skip_hbm,
    inv_hbm,
    w_ref,
    out_ref,
    k_ref,
    v_ref,
    q_ref,
    feat_ref,
    fin_ref,
    bias_ref,
    fout_ref,
    level_ref,
    fwd_ref,
    skip_ref,
    inv_ref,
    load_sem,
    x_buf,
    g_buf,
    w_buf,
    spec,
    acc,
    x_send,
    x_recv,
    g_send,
    g_recv,
    w_send,
    w_recv,
    z_send,
    z_recv,
    own_sem,
):
    rows, cols = q_ref.shape
    length = rows * n_seq
    width = w_buf.shape[1]
    me_seq = lax.axis_index("seq")
    me_chan = lax.axis_index("chan")
    paired = n_chan == 8 and n_seq % 2 == 0
    fetched = {6: 2, 7: 2, 4: 3, 2: 3, 5: 3, 3: 3} if paired else {}

    barrier = pltpu.get_barrier_semaphore()
    for step in range(1, n_seq):
        pl.semaphore_signal(
            barrier, inc=1, device_id={"seq": lax.rem(me_seq + step, n_seq)}, device_id_type=MESH
        )
    for mask in range(1, n_chan):
        pl.semaphore_signal(
            barrier, inc=1, device_id={"chan": flipped(me_chan, mask)}, device_id_type=MESH
        )

    sources = (
        k_hbm, v_hbm, fin_hbm, feat_hbm, bias_hbm, fout_hbm, level_hbm, fwd_hbm, q_hbm, skip_hbm, inv_hbm
    )
    targets = (
        k_ref, v_ref, fin_ref, feat_ref, bias_ref, fout_ref, level_ref, fwd_ref, q_ref, skip_ref, inv_ref
    )
    loads = [
        pltpu.make_async_copy(source, target, load_sem.at[place])
        for place, (source, target) in enumerate(zip(sources, targets))
    ]
    for load in loads:
        load.start()
    own_weight = pltpu.make_async_copy(
        w_ref.at[pl.ds(pl.multiple_of(me_chan * width, width), width)], w_buf.at[0], own_sem
    )
    own_weight.start()
    loads[0].wait()
    loads[1].wait()
    mixed_in = k_ref[...].astype(jnp.float32) * v_ref[...].astype(jnp.float32)
    x_buf[0] = mixed_in.astype(jnp.bfloat16)

    def x_copy(step):
        return pltpu.make_async_remote_copy(
            src_ref=x_buf.at[0],
            dst_ref=x_buf.at[step],
            send_sem=x_send.at[step],
            recv_sem=x_recv.at[step],
            device_id={"seq": lax.rem(me_seq + step, n_seq)},
            device_id_type=MESH,
        )

    piece = width // 4
    odd = lax.rem(me_seq, 2)

    def block_rows(start, count):
        return pl.ds(pl.multiple_of(start, piece), count)

    def w_copy(mask, first=False):
        peer = flipped(me_chan, mask)
        count = (4 - fetched.get(mask, 4)) * piece
        start = count
        if first:
            start = odd * (width - count)
        else:
            count = width - 2 * count
        place = mask + n_chan if first else mask
        return pltpu.make_async_remote_copy(
            src_ref=w_ref.at[block_rows(peer * width + start, count)],
            dst_ref=w_buf.at[mask, block_rows(start, count)],
            send_sem=w_send.at[place],
            recv_sem=w_recv.at[place],
            device_id={"chan": peer},
            device_id_type=MESH,
        )

    def z_copy(mask, arrives=False):
        count = (4 - fetched[mask]) * piece
        side = 1 - odd if arrives else odd
        part = w_buf.at[mask, block_rows(side * (width - count), count)]
        return pltpu.make_async_remote_copy(
            src_ref=part,
            dst_ref=part,
            send_sem=z_send.at[mask],
            recv_sem=z_recv.at[mask],
            device_id={"seq": flipped(me_seq, 1)},
            device_id_type=MESH,
        )

    def g_copy(mask):
        relayed = paired and mask > 1 and mask % 2 == 1
        return pltpu.make_async_remote_copy(
            src_ref=g_buf.at[mask - 1 if relayed else 0],
            dst_ref=g_buf.at[mask],
            send_sem=g_send.at[mask],
            recv_sem=g_recv.at[mask],
            device_id={"chan": flipped(me_chan, 1 if relayed else mask)},
            device_id_type=MESH,
        )

    pl.semaphore_wait(barrier, n_seq + n_chan - 2)
    for step in reversed(range(1, n_seq)):
        pl.when(me_seq + step < n_seq)(lambda step=step: x_copy(step).start())
    for mask in fetched:
        w_copy(mask, True).start()
    kept = [mask for mask in (4, 2, 5, 3, 1) if paired] or list(reversed(range(1, n_chan)))
    for mask in kept:
        w_copy(mask).start()

    def forward(mask):
        w_copy(mask, True).wait_recv()
        z_copy(mask).start()

    for load in loads[2:8]:
        load.wait()
    levels = jnp.maximum(2.0 * level_ref[...] - 1.0, 0.0)
    rate = 0.5 / length * jnp.exp(levels * math.log(length / 16.0))
    row_index = lax.broadcasted_iota(jnp.int32, (rows, cols), 0)
    alternate = (1 - 2 * (row_index % 2)).astype(jnp.float32)
    alternate = jnp.concatenate([alternate, alternate], axis=0)
    decay = jnp.exp(-rate * row_index.astype(jnp.float32))
    decay = jnp.concatenate([decay, decay], axis=1)
    bias = bias_ref[...] * (0.5 / math.pi)
    bias = jnp.concatenate([bias, bias], axis=1)
    first = [twice(term) for term in split(fin_ref[...] * (0.5 / math.pi), 3)]
    first = jnp.concatenate([first[right] for left, right in products], axis=0)
    second = [twice(term) for term in split(fout_ref[...], 2)]
    second = jnp.concatenate([second[0], second[0], second[1]], axis=0)

    def tap_pair(pair, squares):
        turns = jnp.dot(feat_ref[pair], first, preferred_element_type=jnp.float32)
        high, low = split(sin_turns(turns + bias), 2)
        hidden = jnp.concatenate([high, low, high], axis=1)
        raw = jnp.dot(hidden, second, preferred_element_type=jnp.float32)
        starts = [rate * -(rows * (2 * pair + side)) for side in (0, 1)]
        taps = raw * (decay * jnp.exp(jnp.concatenate(starts, axis=1)))
        both = jnp.dot(
            fwd_ref[...], taps.astype(jnp.bfloat16), preferred_element_type=jnp.float32
        )
        early, late = both[:, :cols], both[:, cols:]
        spec[2 * pair] += alternate * early
        spec[2 * pair + 1] = early + alternate * late
        if n_seq <= 4:
            if 2 * pair + 2 < n_seq:
                spec[2 * pair + 2] = late
        else:
            pl.when(2 * pair + 2 < n_seq)(lambda: spec.__setitem__(2 * pair + 2, late))
        return squares + jnp.sum(taps * taps, axis=0, keepdims=True)

    spec[0] = jnp.zeros_like(spec[0])
    squares = jnp.zeros((1, 2 * cols), jnp.float32)
    if n_seq <= 4:
        for pair in range(n_seq // 2):
            squares = tap_pair(pair, squares)
    else:
        squares = lax.fori_loop(0, n_seq // 2, tap_pair, squares)
    scale = lax.rsqrt(squares[:, :cols] + squares[:, cols:] + 1e-05)

    def add_block(step):
        if step > 0:
            x_copy(step).wait_recv()
        field = jnp.dot(fwd_ref[...], x_buf[step], preferred_element_type=jnp.float32)
        x_cos, x_sin = field[:rows], field[rows:]
        h_cos, h_sin = spec[step, :rows], spec[step, rows:]
        terms = (x_cos * h_cos, x_sin * h_sin, x_cos * h_sin + x_sin * h_cos)
        for place, term in enumerate(terms):
            acc[place] = term if step == 0 else acc[place] + term

    for step in range(n_seq):
        if step == 0:
            add_block(step)
            for mask in fetched:
                if mask not in kept:
                    pl.when(odd == 1)(lambda mask=mask: forward(mask))
        else:
            pl.when(me_seq >= step)(lambda step=step: add_block(step))

    for load in loads[8:]:
        load.wait()
    edge = row_index == 0
    y_cos = acc[0] - jnp.where(edge, 0.0, acc[1])
    y_sin = jnp.where(edge, acc[1], acc[2])
    field = jnp.concatenate([y_cos, y_sin], axis=0) * (0.5 / rows)
    convolved = jnp.dot(
        inv_ref[...], field.astype(jnp.bfloat16), preferred_element_type=jnp.float32
    )
    mixed_in = k_ref[...].astype(jnp.float32) * v_ref[...].astype(jnp.float32)
    gated = q_ref[...].astype(jnp.float32) * (convolved * scale + skip_ref[...] * mixed_in)
    g_buf[0] = gated.astype(jnp.bfloat16)
    far = range(2, n_chan, 2 if paired else 1)
    for mask in reversed(far):
        g_copy(mask).start()
    g_copy(1).start()
    for step in range(1, n_seq):
        pl.when(me_seq + step < n_seq)(lambda step=step: x_copy(step).wait_send())
    for mask in fetched:
        if mask in kept:
            forward(mask)
        else:
            pl.when(odd == 0)(lambda mask=mask: forward(mask))
    own_weight.wait()
    total = None
    for pair in range(0, n_chan, 2):
        for mask in (pair, pair + 1):
            if mask == 0:
                continue
            if mask in fetched:
                z_copy(mask, True).wait_recv()
            if mask in kept:
                w_copy(mask).wait_recv()
            if not (paired and mask in far):
                g_copy(mask).wait_recv()
        left = jnp.concatenate([g_buf[pair], g_buf[pair + 1]], axis=1)
        right = jnp.concatenate([w_buf[pair], w_buf[pair + 1]], axis=1)
        product = lax.dot_general(
            left, right, (((1,), (1,)), ((), ())), preferred_element_type=jnp.float32
        )
        total = product if total is None else total + product
        if paired and pair < 4:
            for mask in (2, 4) if pair == 0 else (6,):
                g_copy(mask).wait_recv()
                g_copy(mask + 1).start()
    out_ref[...] = total.astype(out_ref.dtype)

    for mask in fetched:
        z_copy(mask).wait_send()
        w_copy(mask, True).wait_send()
    for mask in range(1, n_chan):
        if mask in kept:
            w_copy(mask).wait_send()
        g_copy(mask).wait_send()


def solution(mesh):
    n_seq, n_chan = mesh.shape["seq"], mesh.shape["chan"]

    def body(query, key, value, fin, bias, fout, level, skip, weight):
        rows, cols = query.shape
        width = weight.shape[0] // n_chan
        forward, inverse = dft_tables(rows)
        features = feature_table(fin.shape[0] // 2, n_seq, rows)
        operands = (
            key,
            value,
            query,
            jnp.asarray(features),
            fin,
            bias.reshape(1, -1),
            fout,
            level.reshape(1, -1),
            jnp.asarray(forward, jnp.bfloat16),
            skip.reshape(1, -1),
            jnp.asarray(inverse, jnp.bfloat16),
        )
        return pl.pallas_call(
            functools.partial(kernel, n_seq, n_chan),
            out_shape=pltpu.VMEM((rows, width), jnp.bfloat16),
            in_specs=[pl.BlockSpec(memory_space=pltpu.HBM)] * (len(operands) + 1),
            out_specs=pl.BlockSpec(memory_space=pltpu.VMEM),
            scratch_shapes=[pltpu.VMEM(item.shape, item.dtype) for item in operands]
            + [
                pltpu.SemaphoreType.DMA((len(operands),)),
                pltpu.VMEM((n_seq, rows, cols), jnp.bfloat16),
                pltpu.VMEM((n_chan, rows, cols), jnp.bfloat16),
                pltpu.VMEM((n_chan, width, cols), jnp.bfloat16),
                pltpu.VMEM((n_seq, 2 * rows, cols), jnp.float32),
                pltpu.VMEM((3, rows, cols), jnp.float32),
                pltpu.SemaphoreType.DMA((n_seq,)),
                pltpu.SemaphoreType.DMA((n_seq,)),
                pltpu.SemaphoreType.DMA((n_chan,)),
                pltpu.SemaphoreType.DMA((n_chan,)),
                pltpu.SemaphoreType.DMA((2 * n_chan,)),
                pltpu.SemaphoreType.DMA((2 * n_chan,)),
                pltpu.SemaphoreType.DMA((n_chan,)),
                pltpu.SemaphoreType.DMA((n_chan,)),
                pltpu.SemaphoreType.DMA,
            ],
            compiler_params=pltpu.CompilerParams(
                collective_id=0, has_side_effects=True, vmem_limit_bytes=63 * 1024 * 1024
            ),
        )(*operands, weight)

    placed = (
        P("seq", "chan"),
        P("seq", "chan"),
        P("seq", "chan"),
        P(),
        P(),
        P(None, "chan"),
        P("chan"),
        P("chan"),
        P(None, "chan"),
    )
    return jax.shard_map(
        body, mesh=mesh, in_specs=placed, out_specs=P("seq", "chan"), check_vma=False
    )
```

```python
import functools
import math

import jax
import jax.numpy as jnp
import ml_dtypes
import numpy as np
from jax import lax
from jax.experimental import pallas as pl
from jax.experimental.pallas import tpu as pltpu
from jax.sharding import PartitionSpec as P

MESH = pl.DeviceIdType.MESH
products = ((0, 0), (0, 1), (1, 0), (0, 2), (1, 1), (2, 0))


def flipped(index, mask):
    bit, result = 1, index
    while bit <= mask:
        if mask & bit:
            result = result + bit - 2 * bit * ((index // bit) % 2)
        bit *= 2
    return result


def dft_tables(rows):
    freq = np.arange(rows)[:, None]
    size = 2 * rows

    def packed(times):
        angles = (freq * times[None, :] % size) * (2.0 * math.pi / size)
        sines = np.sin(angles)
        sines[0] = 1.0 - 2.0 * (times % 2)
        return np.concatenate([np.cos(angles), sines], axis=0)

    forward = packed(np.arange(rows))
    weight = np.full((2 * rows, 1), 2.0 / size)
    weight[0] = weight[rows] = 1.0 / size
    inverse = (packed(np.arange(rows, size)) * weight * size).T
    return forward, inverse


def feature_table(half_count, seq_count, rows):
    length = seq_count * rows
    freq = np.arange(1, half_count + 1)
    phases = (np.arange(length)[:, None] * freq[None, :] % length) * (2.0 * math.pi / length)
    table = np.concatenate([np.sin(phases), np.cos(phases)], axis=1).astype(np.float32)
    table = table.reshape(seq_count // 2, 2, rows, 2 * half_count)
    table = np.concatenate([table[:, 0], table[:, 1]], axis=2)
    terms = []
    for unused in range(3):
        terms.append(table.astype(ml_dtypes.bfloat16))
        table = table - terms[-1].astype(np.float32)
    return np.concatenate([terms[left] for left, right in products], axis=2)


def split(value, count):
    terms = []
    for place in range(count):
        terms.append(value.astype(jnp.bfloat16))
        if place + 1 < count:
            value = value - terms[-1].astype(jnp.float32)
    return terms


def twice(block):
    empty = jnp.zeros_like(block)
    return jnp.concatenate(
        [jnp.concatenate([block, empty], axis=1), jnp.concatenate([empty, block], axis=1)], axis=0
    )


def sin_turns(turns):
    angle = (turns - jnp.round(turns)) * (2.0 * math.pi)
    square = angle * angle
    total = jnp.full_like(angle, 1.0 / math.factorial(17))
    for order in (15, 13, 11, 9, 7, 5, 3, 1):
        sign = -1.0 if order % 4 == 3 else 1.0
        total = total * square + sign / math.factorial(order)
    return total * angle


def kernel(
    n_seq,
    n_chan,
    k_hbm,
    v_hbm,
    q_hbm,
    feat_hbm,
    fin_hbm,
    bias_hbm,
    fout_hbm,
    level_hbm,
    fwd_hbm,
    skip_hbm,
    inv_hbm,
    w_ref,
    out_ref,
    k_ref,
    v_ref,
    q_ref,
    feat_ref,
    fin_ref,
    bias_ref,
    fout_ref,
    level_ref,
    fwd_ref,
    skip_ref,
    inv_ref,
    load_sem,
    x_buf,
    g_buf,
    w_buf,
    spec,
    acc,
    x_send,
    x_recv,
    g_send,
    g_recv,
    w_send,
    w_recv,
    z_send,
    z_recv,
    own_sem,
):
    rows, cols = q_ref.shape
    length = rows * n_seq
    width = w_buf.shape[1]
    me_seq = lax.axis_index("seq")
    me_chan = lax.axis_index("chan")
    paired = n_chan == 8 and n_seq % 2 == 0
    fetched = {6: 2, 7: 2, 4: 3, 2: 3, 5: 3, 3: 3} if paired else {}

    barrier = pltpu.get_barrier_semaphore()
    for step in range(1, n_seq):
        pl.semaphore_signal(
            barrier, inc=1, device_id={"seq": lax.rem(me_seq + step, n_seq)}, device_id_type=MESH
        )
    for mask in range(1, n_chan):
        pl.semaphore_signal(
            barrier, inc=1, device_id={"chan": flipped(me_chan, mask)}, device_id_type=MESH
        )

    sources = (
        k_hbm, v_hbm, fin_hbm, feat_hbm, bias_hbm, fout_hbm, level_hbm, fwd_hbm, q_hbm, skip_hbm, inv_hbm
    )
    targets = (
        k_ref, v_ref, fin_ref, feat_ref, bias_ref, fout_ref, level_ref, fwd_ref, q_ref, skip_ref, inv_ref
    )
    loads = [
        pltpu.make_async_copy(source, target, load_sem.at[place])
        for place, (source, target) in enumerate(zip(sources, targets))
    ]
    for load in loads:
        load.start()
    own_weight = pltpu.make_async_copy(
        w_ref.at[pl.ds(pl.multiple_of(me_chan * width, width), width)], w_buf.at[0], own_sem
    )
    own_weight.start()
    loads[0].wait()
    loads[1].wait()
    mixed_in = k_ref[...].astype(jnp.float32) * v_ref[...].astype(jnp.float32)
    x_buf[0] = mixed_in.astype(jnp.bfloat16)

    def x_copy(step):
        return pltpu.make_async_remote_copy(
            src_ref=x_buf.at[0],
            dst_ref=x_buf.at[step],
            send_sem=x_send.at[step],
            recv_sem=x_recv.at[step],
            device_id={"seq": lax.rem(me_seq + step, n_seq)},
            device_id_type=MESH,
        )

    piece = width // 4
    odd = lax.rem(me_seq, 2)

    def block_rows(start, count):
        return pl.ds(pl.multiple_of(start, piece), count)

    def w_copy(mask, first=False):
        peer = flipped(me_chan, mask)
        count = (4 - fetched.get(mask, 4)) * piece
        start = count
        if first:
            start = odd * (width - count)
        else:
            count = width - 2 * count
        place = mask + n_chan if first else mask
        return pltpu.make_async_remote_copy(
            src_ref=w_ref.at[block_rows(peer * width + start, count)],
            dst_ref=w_buf.at[mask, block_rows(start, count)],
            send_sem=w_send.at[place],
            recv_sem=w_recv.at[place],
            device_id={"chan": peer},
            device_id_type=MESH,
        )

    def z_copy(mask, arrives=False):
        count = (4 - fetched[mask]) * piece
        side = 1 - odd if arrives else odd
        part = w_buf.at[mask, block_rows(side * (width - count), count)]
        return pltpu.make_async_remote_copy(
            src_ref=part,
            dst_ref=part,
            send_sem=z_send.at[mask],
            recv_sem=z_recv.at[mask],
            device_id={"seq": flipped(me_seq, 1)},
            device_id_type=MESH,
        )

    def g_copy(mask):
        relayed = paired and mask > 1 and mask % 2 == 1
        return pltpu.make_async_remote_copy(
            src_ref=g_buf.at[mask - 1 if relayed else 0],
            dst_ref=g_buf.at[mask],
            send_sem=g_send.at[mask],
            recv_sem=g_recv.at[mask],
            device_id={"chan": flipped(me_chan, 1 if relayed else mask)},
            device_id_type=MESH,
        )

    pl.semaphore_wait(barrier, n_seq + n_chan - 2)
    for step in reversed(range(1, n_seq)):
        pl.when(me_seq + step < n_seq)(lambda step=step: x_copy(step).start())
    for mask in fetched:
        w_copy(mask, True).start()
    kept = [mask for mask in (4, 2, 5, 3, 1) if paired] or list(reversed(range(1, n_chan)))
    for mask in kept:
        w_copy(mask).start()

    def forward(mask):
        w_copy(mask, True).wait_recv()
        z_copy(mask).start()

    for load in loads[2:8]:
        load.wait()
    levels = jnp.maximum(2.0 * level_ref[...] - 1.0, 0.0)
    rate = 0.5 / length * jnp.exp(levels * math.log(length / 16.0))
    row_index = lax.broadcasted_iota(jnp.int32, (rows, cols), 0)
    alternate = (1 - 2 * (row_index % 2)).astype(jnp.float32)
    alternate = jnp.concatenate([alternate, alternate], axis=0)
    decay = jnp.exp(-rate * row_index.astype(jnp.float32))
    decay = jnp.concatenate([decay, decay], axis=1)
    bias = bias_ref[...] * (0.5 / math.pi)
    bias = jnp.concatenate([bias, bias], axis=1)
    first = [twice(term) for term in split(fin_ref[...] * (0.5 / math.pi), 3)]
    first = jnp.concatenate([first[right] for left, right in products], axis=0)
    second = [twice(term) for term in split(fout_ref[...], 2)]
    second = jnp.concatenate([second[0], second[0], second[1]], axis=0)

    def tap_pair(pair, squares):
        turns = jnp.dot(feat_ref[pair], first, preferred_element_type=jnp.float32)
        high, low = split(sin_turns(turns + bias), 2)
        hidden = jnp.concatenate([high, low, high], axis=1)
        raw = jnp.dot(hidden, second, preferred_element_type=jnp.float32)
        starts = [rate * -(rows * (2 * pair + side)) for side in (0, 1)]
        taps = raw * (decay * jnp.exp(jnp.concatenate(starts, axis=1)))
        both = jnp.dot(
            fwd_ref[...], taps.astype(jnp.bfloat16), preferred_element_type=jnp.float32
        )
        early, late = both[:, :cols], both[:, cols:]
        spec[2 * pair] += alternate * early
        spec[2 * pair + 1] = early + alternate * late
        if n_seq <= 4:
            if 2 * pair + 2 < n_seq:
                spec[2 * pair + 2] = late
        else:
            pl.when(2 * pair + 2 < n_seq)(lambda: spec.__setitem__(2 * pair + 2, late))
        return squares + jnp.sum(taps * taps, axis=0, keepdims=True)

    spec[0] = jnp.zeros_like(spec[0])
    squares = jnp.zeros((1, 2 * cols), jnp.float32)
    if n_seq <= 4:
        for pair in range(n_seq // 2):
            squares = tap_pair(pair, squares)
    else:
        squares = lax.fori_loop(0, n_seq // 2, tap_pair, squares)
    scale = lax.rsqrt(squares[:, :cols] + squares[:, cols:] + 1e-05)

    def add_block(step):
        if step > 0:
            x_copy(step).wait_recv()
        field = jnp.dot(fwd_ref[...], x_buf[step], preferred_element_type=jnp.float32)
        x_cos, x_sin = field[:rows], field[rows:]
        h_cos, h_sin = spec[step, :rows], spec[step, rows:]
        terms = (x_cos * h_cos, x_sin * h_sin, x_cos * h_sin + x_sin * h_cos)
        for place, term in enumerate(terms):
            acc[place] = term if step == 0 else acc[place] + term

    for step in range(n_seq):
        if step == 0:
            add_block(step)
            for mask in fetched:
                forward(mask)
        else:
            pl.when(me_seq >= step)(lambda step=step: add_block(step))

    for load in loads[8:]:
        load.wait()
    edge = row_index == 0
    y_cos = acc[0] - jnp.where(edge, 0.0, acc[1])
    y_sin = jnp.where(edge, acc[1], acc[2])
    field = jnp.concatenate([y_cos, y_sin], axis=0) * (0.5 / rows)
    convolved = jnp.dot(
        inv_ref[...], field.astype(jnp.bfloat16), preferred_element_type=jnp.float32
    )
    mixed_in = k_ref[...].astype(jnp.float32) * v_ref[...].astype(jnp.float32)
    gated = q_ref[...].astype(jnp.float32) * (convolved * scale + skip_ref[...] * mixed_in)
    g_buf[0] = gated.astype(jnp.bfloat16)
    far = range(2, n_chan, 2 if paired else 1)
    for mask in reversed(far):
        g_copy(mask).start()
    g_copy(1).start()
    for step in range(1, n_seq):
        pl.when(me_seq + step < n_seq)(lambda step=step: x_copy(step).wait_send())
    own_weight.wait()
    total = None
    for pair in range(0, n_chan, 2):
        for mask in (pair, pair + 1):
            if mask == 0:
                continue
            if mask in fetched:
                z_copy(mask, True).wait_recv()
            if mask in kept:
                w_copy(mask).wait_recv()
            if not (paired and mask in far):
                g_copy(mask).wait_recv()
        left = jnp.concatenate([g_buf[pair], g_buf[pair + 1]], axis=1)
        right = jnp.concatenate([w_buf[pair], w_buf[pair + 1]], axis=1)
        product = lax.dot_general(
            left, right, (((1,), (1,)), ((), ())), preferred_element_type=jnp.float32
        )
        total = product if total is None else total + product
        if paired and pair == 0:
            for mask in far:
                g_copy(mask).wait_recv()
                g_copy(mask + 1).start()
    out_ref[...] = total.astype(out_ref.dtype)

    for mask in fetched:
        z_copy(mask).wait_send()
        w_copy(mask, True).wait_send()
    for mask in range(1, n_chan):
        if mask in kept:
            w_copy(mask).wait_send()
        g_copy(mask).wait_send()


def solution(mesh):
    n_seq, n_chan = mesh.shape["seq"], mesh.shape["chan"]

    def body(query, key, value, fin, bias, fout, level, skip, weight):
        rows, cols = query.shape
        width = weight.shape[0] // n_chan
        forward, inverse = dft_tables(rows)
        features = feature_table(fin.shape[0] // 2, n_seq, rows)
        operands = (
            key,
            value,
            query,
            jnp.asarray(features),
            fin,
            bias.reshape(1, -1),
            fout,
            level.reshape(1, -1),
            jnp.asarray(forward, jnp.bfloat16),
            skip.reshape(1, -1),
            jnp.asarray(inverse, jnp.bfloat16),
        )
        return pl.pallas_call(
            functools.partial(kernel, n_seq, n_chan),
            out_shape=pltpu.VMEM((rows, width), jnp.bfloat16),
            in_specs=[pl.BlockSpec(memory_space=pltpu.HBM)] * (len(operands) + 1),
            out_specs=pl.BlockSpec(memory_space=pltpu.VMEM),
            scratch_shapes=[pltpu.VMEM(item.shape, item.dtype) for item in operands]
            + [
                pltpu.SemaphoreType.DMA((len(operands),)),
                pltpu.VMEM((n_seq, rows, cols), jnp.bfloat16),
                pltpu.VMEM((n_chan, rows, cols), jnp.bfloat16),
                pltpu.VMEM((n_chan, width, cols), jnp.bfloat16),
                pltpu.VMEM((n_seq, 2 * rows, cols), jnp.float32),
                pltpu.VMEM((3, rows, cols), jnp.float32),
                pltpu.SemaphoreType.DMA((n_seq,)),
                pltpu.SemaphoreType.DMA((n_seq,)),
                pltpu.SemaphoreType.DMA((n_chan,)),
                pltpu.SemaphoreType.DMA((n_chan,)),
                pltpu.SemaphoreType.DMA((2 * n_chan,)),
                pltpu.SemaphoreType.DMA((2 * n_chan,)),
                pltpu.SemaphoreType.DMA((n_chan,)),
                pltpu.SemaphoreType.DMA((n_chan,)),
                pltpu.SemaphoreType.DMA,
            ],
            compiler_params=pltpu.CompilerParams(
                collective_id=0, has_side_effects=True, vmem_limit_bytes=63 * 1024 * 1024
            ),
        )(*operands, weight)

    placed = (
        P("seq", "chan"),
        P("seq", "chan"),
        P("seq", "chan"),
        P(),
        P(),
        P(None, "chan"),
        P("chan"),
        P("chan"),
        P(None, "chan"),
    )
    return jax.shard_map(
        body, mesh=mesh, in_specs=placed, out_specs=P("seq", "chan"), check_vma=False
    )
```

```python
import functools
import math

import jax
import jax.numpy as jnp
import ml_dtypes
import numpy as np
from jax import lax
from jax.experimental import pallas as pl
from jax.experimental.pallas import tpu as pltpu
from jax.sharding import PartitionSpec as P

MESH = pl.DeviceIdType.MESH
products = ((0, 0), (0, 1), (1, 0), (0, 2), (1, 1), (2, 0))


def flipped(index, mask):
    bit, result = 1, index
    while bit <= mask:
        if mask & bit:
            result = result + bit - 2 * bit * ((index // bit) % 2)
        bit *= 2
    return result


def dft_tables(rows):
    freq = np.arange(rows)[:, None]
    size = 2 * rows

    def packed(times):
        angles = (freq * times[None, :] % size) * (2.0 * math.pi / size)
        sines = np.sin(angles)
        sines[0] = 1.0 - 2.0 * (times % 2)
        return np.concatenate([np.cos(angles), sines], axis=0)

    forward = packed(np.arange(rows))
    weight = np.full((2 * rows, 1), 2.0 / size)
    weight[0] = weight[rows] = 1.0 / size
    inverse = (packed(np.arange(rows, size)) * weight * size).T
    return forward, inverse


def feature_table(half_count, seq_count, rows):
    length = seq_count * rows
    freq = np.arange(1, half_count + 1)
    phases = (np.arange(length)[:, None] * freq[None, :] % length) * (2.0 * math.pi / length)
    table = np.concatenate([np.sin(phases), np.cos(phases)], axis=1).astype(np.float32)
    table = table.reshape(seq_count // 2, 2, rows, 2 * half_count)
    table = np.concatenate([table[:, 0], table[:, 1]], axis=2)
    terms = []
    for unused in range(3):
        terms.append(table.astype(ml_dtypes.bfloat16))
        table = table - terms[-1].astype(np.float32)
    return np.concatenate([terms[left] for left, right in products], axis=2)


def split(value, count):
    terms = []
    for place in range(count):
        terms.append(value.astype(jnp.bfloat16))
        if place + 1 < count:
            value = value - terms[-1].astype(jnp.float32)
    return terms


def twice(block):
    empty = jnp.zeros_like(block)
    return jnp.concatenate(
        [jnp.concatenate([block, empty], axis=1), jnp.concatenate([empty, block], axis=1)], axis=0
    )


def sin_turns(turns):
    angle = (turns - jnp.round(turns)) * (2.0 * math.pi)
    square = angle * angle
    total = jnp.full_like(angle, 1.0 / math.factorial(17))
    for order in (15, 13, 11, 9, 7, 5, 3, 1):
        sign = -1.0 if order % 4 == 3 else 1.0
        total = total * square + sign / math.factorial(order)
    return total * angle


def kernel(
    n_seq,
    n_chan,
    k_hbm,
    v_hbm,
    q_hbm,
    feat_hbm,
    fin_hbm,
    bias_hbm,
    fout_hbm,
    level_hbm,
    fwd_hbm,
    skip_hbm,
    inv_hbm,
    w_ref,
    out_ref,
    k_ref,
    v_ref,
    q_ref,
    feat_ref,
    fin_ref,
    bias_ref,
    fout_ref,
    level_ref,
    fwd_ref,
    skip_ref,
    inv_ref,
    load_sem,
    x_buf,
    g_buf,
    w_buf,
    spec,
    acc,
    x_send,
    x_recv,
    g_send,
    g_recv,
    w_send,
    w_recv,
    z_send,
    z_recv,
    own_sem,
):
    rows, cols = q_ref.shape
    length = rows * n_seq
    width = w_buf.shape[1]
    me_seq = lax.axis_index("seq")
    me_chan = lax.axis_index("chan")
    paired = n_chan == 8 and n_seq % 2 == 0
    fetched = {6: 2, 7: 2, 4: 3, 2: 3, 5: 3, 3: 3} if paired else {}

    barrier = pltpu.get_barrier_semaphore()
    for step in range(1, n_seq):
        pl.semaphore_signal(
            barrier, inc=1, device_id={"seq": lax.rem(me_seq + step, n_seq)}, device_id_type=MESH
        )
    for mask in range(1, n_chan):
        pl.semaphore_signal(
            barrier, inc=1, device_id={"chan": flipped(me_chan, mask)}, device_id_type=MESH
        )

    sources = (
        k_hbm, v_hbm, fin_hbm, feat_hbm, bias_hbm, fout_hbm, level_hbm, fwd_hbm, q_hbm, skip_hbm, inv_hbm
    )
    targets = (
        k_ref, v_ref, fin_ref, feat_ref, bias_ref, fout_ref, level_ref, fwd_ref, q_ref, skip_ref, inv_ref
    )
    loads = [
        pltpu.make_async_copy(source, target, load_sem.at[place])
        for place, (source, target) in enumerate(zip(sources, targets))
    ]
    for load in loads:
        load.start()
    own_weight = pltpu.make_async_copy(
        w_ref.at[pl.ds(pl.multiple_of(me_chan * width, width), width)], w_buf.at[0], own_sem
    )
    own_weight.start()
    loads[0].wait()
    loads[1].wait()
    mixed_in = k_ref[...].astype(jnp.float32) * v_ref[...].astype(jnp.float32)
    x_buf[0] = mixed_in.astype(jnp.bfloat16)

    def x_copy(step):
        return pltpu.make_async_remote_copy(
            src_ref=x_buf.at[0],
            dst_ref=x_buf.at[step],
            send_sem=x_send.at[step],
            recv_sem=x_recv.at[step],
            device_id={"seq": lax.rem(me_seq + step, n_seq)},
            device_id_type=MESH,
        )

    piece = width // 4
    odd = lax.rem(me_seq, 2)

    def block_rows(start, count):
        return pl.ds(pl.multiple_of(start, piece), count)

    def w_copy(mask, first=False):
        peer = flipped(me_chan, mask)
        count = (4 - fetched.get(mask, 4)) * piece
        start = count
        if first:
            start = odd * (width - count)
        else:
            count = width - 2 * count
        place = mask + n_chan if first else mask
        return pltpu.make_async_remote_copy(
            src_ref=w_ref.at[block_rows(peer * width + start, count)],
            dst_ref=w_buf.at[mask, block_rows(start, count)],
            send_sem=w_send.at[place],
            recv_sem=w_recv.at[place],
            device_id={"chan": peer},
            device_id_type=MESH,
        )

    def z_copy(mask, arrives=False):
        count = (4 - fetched[mask]) * piece
        side = 1 - odd if arrives else odd
        part = w_buf.at[mask, block_rows(side * (width - count), count)]
        return pltpu.make_async_remote_copy(
            src_ref=part,
            dst_ref=part,
            send_sem=z_send.at[mask],
            recv_sem=z_recv.at[mask],
            device_id={"seq": flipped(me_seq, 1)},
            device_id_type=MESH,
        )

    def g_copy(mask):
        relayed = paired and mask > 1 and mask % 2 == 1
        return pltpu.make_async_remote_copy(
            src_ref=g_buf.at[mask - 1 if relayed else 0],
            dst_ref=g_buf.at[mask],
            send_sem=g_send.at[mask],
            recv_sem=g_recv.at[mask],
            device_id={"chan": flipped(me_chan, 1 if relayed else mask)},
            device_id_type=MESH,
        )

    pl.semaphore_wait(barrier, n_seq + n_chan - 2)
    for step in reversed(range(1, n_seq)):
        pl.when(me_seq + step < n_seq)(lambda step=step: x_copy(step).start())
    for mask in fetched:
        w_copy(mask, True).start()
    kept = [mask for mask in (4, 2, 5, 3, 1) if paired] or list(reversed(range(1, n_chan)))
    for mask in kept:
        w_copy(mask).start()

    def forward(mask):
        w_copy(mask, True).wait_recv()
        z_copy(mask).start()

    for load in loads[2:8]:
        load.wait()
    levels = jnp.maximum(2.0 * level_ref[...] - 1.0, 0.0)
    rate = 0.5 / length * jnp.exp(levels * math.log(length / 16.0))
    row_index = lax.broadcasted_iota(jnp.int32, (rows, cols), 0)
    alternate = (1 - 2 * (row_index % 2)).astype(jnp.float32)
    alternate = jnp.concatenate([alternate, alternate], axis=0)
    decay = jnp.exp(-rate * row_index.astype(jnp.float32))
    decay = jnp.concatenate([decay, decay], axis=1)
    bias = bias_ref[...] * (0.5 / math.pi)
    bias = jnp.concatenate([bias, bias], axis=1)
    first = [twice(term) for term in split(fin_ref[...] * (0.5 / math.pi), 3)]
    first = jnp.concatenate([first[right] for left, right in products], axis=0)
    second = [twice(term) for term in split(fout_ref[...], 2)]
    second = jnp.concatenate([second[0], second[0], second[1]], axis=0)

    def tap_pair(pair, squares):
        turns = jnp.dot(feat_ref[pair], first, preferred_element_type=jnp.float32)
        high, low = split(sin_turns(turns + bias), 2)
        hidden = jnp.concatenate([high, low, high], axis=1)
        raw = jnp.dot(hidden, second, preferred_element_type=jnp.float32)
        starts = [rate * -(rows * (2 * pair + side)) for side in (0, 1)]
        taps = raw * (decay * jnp.exp(jnp.concatenate(starts, axis=1)))
        both = jnp.dot(
            fwd_ref[...], taps.astype(jnp.bfloat16), preferred_element_type=jnp.float32
        )
        early, late = both[:, :cols], both[:, cols:]
        spec[2 * pair] += alternate * early
        spec[2 * pair + 1] = early + alternate * late
        if n_seq <= 4:
            if 2 * pair + 2 < n_seq:
                spec[2 * pair + 2] = late
        else:
            pl.when(2 * pair + 2 < n_seq)(lambda: spec.__setitem__(2 * pair + 2, late))
        return squares + jnp.sum(taps * taps, axis=0, keepdims=True)

    spec[0] = jnp.zeros_like(spec[0])
    squares = jnp.zeros((1, 2 * cols), jnp.float32)
    if n_seq <= 4:
        for pair in range(n_seq // 2):
            squares = tap_pair(pair, squares)
    else:
        squares = lax.fori_loop(0, n_seq // 2, tap_pair, squares)
    scale = lax.rsqrt(squares[:, :cols] + squares[:, cols:] + 1e-05)

    def add_block(step):
        if step > 0:
            x_copy(step).wait_recv()
        field = jnp.dot(fwd_ref[...], x_buf[step], preferred_element_type=jnp.float32)
        x_cos, x_sin = field[:rows], field[rows:]
        h_cos, h_sin = spec[step, :rows], spec[step, rows:]
        terms = (x_cos * h_cos, x_sin * h_sin, x_cos * h_sin + x_sin * h_cos)
        for place, term in enumerate(terms):
            acc[place] = term if step == 0 else acc[place] + term

    for step in range(n_seq):
        if step == 0:
            add_block(step)
            for mask in fetched:
                if mask not in kept:
                    pl.when(odd == 1)(lambda mask=mask: forward(mask))
        else:
            pl.when(me_seq >= step)(lambda step=step: add_block(step))

    for load in loads[8:]:
        load.wait()
    edge = row_index == 0
    y_cos = acc[0] - jnp.where(edge, 0.0, acc[1])
    y_sin = jnp.where(edge, acc[1], acc[2])
    field = jnp.concatenate([y_cos, y_sin], axis=0) * (0.5 / rows)
    convolved = jnp.dot(
        inv_ref[...], field.astype(jnp.bfloat16), preferred_element_type=jnp.float32
    )
    mixed_in = k_ref[...].astype(jnp.float32) * v_ref[...].astype(jnp.float32)
    gated = q_ref[...].astype(jnp.float32) * (convolved * scale + skip_ref[...] * mixed_in)
    g_buf[0] = gated.astype(jnp.bfloat16)
    far = range(2, n_chan, 2 if paired else 1)
    for mask in reversed(far):
        g_copy(mask).start()
    g_copy(1).start()
    for step in range(1, n_seq):
        pl.when(me_seq + step < n_seq)(lambda step=step: x_copy(step).wait_send())
    for mask in fetched:
        if mask in kept:
            forward(mask)
        else:
            pl.when(odd == 0)(lambda mask=mask: forward(mask))
    if paired:
        for mask in far:
            g_copy(mask).wait_recv()
            g_copy(mask + 1).start()
    own_weight.wait()
    total = None
    for pair in range(0, n_chan, 2):
        for mask in (pair, pair + 1):
            if mask == 0:
                continue
            if mask in fetched:
                z_copy(mask, True).wait_recv()
            if mask in kept:
                w_copy(mask).wait_recv()
            if not (paired and mask in far):
                g_copy(mask).wait_recv()
        left = jnp.concatenate([g_buf[pair], g_buf[pair + 1]], axis=1)
        right = jnp.concatenate([w_buf[pair], w_buf[pair + 1]], axis=1)
        product = lax.dot_general(
            left, right, (((1,), (1,)), ((), ())), preferred_element_type=jnp.float32
        )
        total = product if total is None else total + product
    out_ref[...] = total.astype(out_ref.dtype)

    for mask in fetched:
        z_copy(mask).wait_send()
        w_copy(mask, True).wait_send()
    for mask in range(1, n_chan):
        if mask in kept:
            w_copy(mask).wait_send()
        g_copy(mask).wait_send()


def solution(mesh):
    n_seq, n_chan = mesh.shape["seq"], mesh.shape["chan"]

    def body(query, key, value, fin, bias, fout, level, skip, weight):
        rows, cols = query.shape
        width = weight.shape[0] // n_chan
        forward, inverse = dft_tables(rows)
        features = feature_table(fin.shape[0] // 2, n_seq, rows)
        operands = (
            key,
            value,
            query,
            jnp.asarray(features),
            fin,
            bias.reshape(1, -1),
            fout,
            level.reshape(1, -1),
            jnp.asarray(forward, jnp.bfloat16),
            skip.reshape(1, -1),
            jnp.asarray(inverse, jnp.bfloat16),
        )
        return pl.pallas_call(
            functools.partial(kernel, n_seq, n_chan),
            out_shape=pltpu.VMEM((rows, width), jnp.bfloat16),
            in_specs=[pl.BlockSpec(memory_space=pltpu.HBM)] * (len(operands) + 1),
            out_specs=pl.BlockSpec(memory_space=pltpu.VMEM),
            scratch_shapes=[pltpu.VMEM(item.shape, item.dtype) for item in operands]
            + [
                pltpu.SemaphoreType.DMA((len(operands),)),
                pltpu.VMEM((n_seq, rows, cols), jnp.bfloat16),
                pltpu.VMEM((n_chan, rows, cols), jnp.bfloat16),
                pltpu.VMEM((n_chan, width, cols), jnp.bfloat16),
                pltpu.VMEM((n_seq, 2 * rows, cols), jnp.float32),
                pltpu.VMEM((3, rows, cols), jnp.float32),
                pltpu.SemaphoreType.DMA((n_seq,)),
                pltpu.SemaphoreType.DMA((n_seq,)),
                pltpu.SemaphoreType.DMA((n_chan,)),
                pltpu.SemaphoreType.DMA((n_chan,)),
                pltpu.SemaphoreType.DMA((2 * n_chan,)),
                pltpu.SemaphoreType.DMA((2 * n_chan,)),
                pltpu.SemaphoreType.DMA((n_chan,)),
                pltpu.SemaphoreType.DMA((n_chan,)),
                pltpu.SemaphoreType.DMA,
            ],
            compiler_params=pltpu.CompilerParams(
                collective_id=0, has_side_effects=True, vmem_limit_bytes=63 * 1024 * 1024
            ),
        )(*operands, weight)

    placed = (
        P("seq", "chan"),
        P("seq", "chan"),
        P("seq", "chan"),
        P(),
        P(),
        P(None, "chan"),
        P("chan"),
        P("chan"),
        P(None, "chan"),
    )
    return jax.shard_map(
        body, mesh=mesh, in_specs=placed, out_specs=P("seq", "chan"), check_vma=False
    )
```
